128 devices in a mesh: gx: 4 (over z), gy: 32 (over x, y, core).
Axes of the slice: x: 4, y: 4, z: 4, core: 2. Of those that a mesh axis runs over, the one named last changes fastest.
Arguments:
- leaf_multipole: bfloat16 [152, 32768], P(None, ('gx', 'gy')), may hold values from -6 to 6
- up_matrices: bfloat16 [8, 152, 152], replicated, may hold values from -0.15625 to 0.15625
- down_matrices: bfloat16 [8, 152, 152], replicated, may hold values from -0.5 to 0.5
- far_matrices: bfloat16 [316, 152, 152], replicated, may hold values from -0.02734375 to 0.02734375
- send_leaf: int32 [32768], P(('gx', 'gy')), may hold values from 0 to 255
- send_parent: int32 [4096], P(('gx', 'gy')), may hold values from 0 to 31
- codes_leaf: int32 [316, 32768], P(None, ('gx', 'gy')), may hold values from 0 to 2047
- valid_leaf: int32 [316, 32768], P(None, ('gx', 'gy')), may hold values 0 or 1
- codes_parent: int32 [316, 4096], P(None, ('gx', 'gy')), may hold values from 0 to 255
- valid_parent: int32 [316, 4096], P(None, ('gx', 'gy')), may hold values 0 or 1
- codes_coarse: int32 [316, 512], P(None, ('gx', 'gy')), may hold values from 0 to 511
- valid_coarse: int32 [316, 512], P(None, ('gx', 'gy')), may hold values 0 or 1
Outputs:
- far_local: float32 [152, 32768], P(None, ('gx', 'gy'))
The draws below stay inside these ranges and needn't reach their ends.
Inputs may be any that keep to these rules, and one draw needn't show every extreme that they name: `send_leaf`: local box indices of the sending device. `send_parent`: local box indices of the sending device. `codes_leaf`: columns of the target's own device's source table. `codes_parent`: columns of the target's own device's source table.
All inputs are finite; a program needn't handle non-finite values. No bound on the sum of `valid_leaf` or of `valid_parent` or of `valid_coarse` on one device may be relied on, other than what follows from the above.
Results may differ from the reference program's by a relative error of at most 0.0033.
Values may be sent and summed in bfloat16 or wider, within the bound.
No kernel may reach another device: no remote copies, remote signals or barrier semaphores. Data moves between devices by JAX's collectives and lax.ppermute only.
A program may use at most 192 MiB of HBM per device.

```python
import jax
import jax.numpy as jnp
from jax import lax

P_SIZE = 152
NOFF = 316
LEAF_DEV = 256
PARENT_DEV = 32
COARSE_DEV = 4
NBITS = 7
LEAVES = 32768
PARENTS = 4096
COARSE = 512
LEAF_CODES = 2048
PARENT_CODES = 256
N_GX = 4
N_GY = 32


def with_ends(values, own_key, least, top_value):
    longest = values.shape.index(max(values.shape))
    spots = []
    for shift in (0, 1):
        where = [jax.random.randint(jax.random.fold_in(own_key, axis), (), 0, length) for axis, length in enumerate(values.shape)]
        where[longest] = (where[longest] + shift) % values.shape[longest]
        spots.append(tuple(where))
    return values.at[spots[0]].set(least).at[spots[1]].set(top_value)


def block_levels(stream_key, dims, split, low, high):
    factor_of, own = 1.0, jax.random.fold_in(stream_key, 6)
    for axis_at, shards_of in split:
        heights = jnp.exp(jax.random.uniform(jax.random.fold_in(own, axis_at), (shards_of,), jnp.float32, low / len(split), high / len(split)))
        factor_of = factor_of * jnp.repeat(heights, dims[axis_at] // shards_of).reshape([-1 if axis == axis_at else 1 for axis in range(len(dims))])
    return factor_of


def gaussian(own_key, shape, scale, most, cuts=(), kind=jnp.bfloat16):
    drawn = scale * jax.random.normal(own_key, shape, jnp.float32)
    if cuts:
        drawn = drawn * block_levels(own_key, shape, cuts, -0.22, 0.18)
    return jnp.clip(drawn, -most, most).astype(kind)


def setup_inputs(seed: int = 0) -> dict:
    seeds = jax.random.split(jax.random.key(seed), 13)
    leaf_multipole = gaussian(seeds[0], (P_SIZE, LEAVES), 1.0, 6.0, ((1, 128),))
    up_matrices = gaussian(seeds[1], (8, P_SIZE, P_SIZE), (8 * P_SIZE) ** -0.5, 0.15625)
    down_matrices = gaussian(seeds[2], (8, P_SIZE, P_SIZE), P_SIZE ** -0.5, 0.5)
    far_matrices = gaussian(seeds[3], (NOFF, P_SIZE, P_SIZE), (NOFF * P_SIZE) ** -0.5, 0.02734375)
    send_leaf = with_ends(jax.random.randint(seeds[4], (LEAVES,), 0, LEAF_DEV), jax.random.fold_in(seeds[4], 1), 0, LEAF_DEV - 1).astype(jnp.int32)
    send_parent = with_ends(jax.random.randint(seeds[5], (PARENTS,), 0, PARENT_DEV), jax.random.fold_in(seeds[5], 1), 0, PARENT_DEV - 1).astype(jnp.int32)
    codes_leaf = with_ends(jax.random.randint(seeds[6], (NOFF, LEAVES), 0, LEAF_CODES), jax.random.fold_in(seeds[6], 1), 0, LEAF_CODES - 1).astype(jnp.int32)
    valid_leaf = with_ends((jax.random.randint(seeds[7], (NOFF, LEAVES), 0, 5) < 3).astype(jnp.int32), jax.random.fold_in(seeds[7], 1), 0, 1)
    codes_parent = with_ends(jax.random.randint(seeds[8], (NOFF, PARENTS), 0, PARENT_CODES), jax.random.fold_in(seeds[8], 1), 0, PARENT_CODES - 1).astype(jnp.int32)
    valid_parent = with_ends((jax.random.randint(seeds[9], (NOFF, PARENTS), 0, 5) < 3).astype(jnp.int32), jax.random.fold_in(seeds[9], 1), 0, 1)
    codes_coarse = with_ends(jax.random.randint(seeds[10], (NOFF, COARSE), 0, COARSE), jax.random.fold_in(seeds[10], 1), 0, COARSE - 1).astype(jnp.int32)
    valid_coarse = with_ends((jax.random.randint(seeds[11], (NOFF, COARSE), 0, 5) < 3).astype(jnp.int32), jax.random.fold_in(seeds[11], 1), 0, 1)
    return {"leaf_multipole": leaf_multipole, "up_matrices": up_matrices, "down_matrices": down_matrices, "far_matrices": far_matrices, "send_leaf": send_leaf, "send_parent": send_parent, "codes_leaf": codes_leaf, "valid_leaf": valid_leaf, "codes_parent": codes_parent, "valid_parent": valid_parent, "codes_coarse": codes_coarse, "valid_coarse": valid_coarse}


def upward(matrices, children, groups):
    devices = N_GX * N_GY
    shaped = children.astype(jnp.float32).reshape(P_SIZE, devices, 8, groups)
    parents = jnp.einsum("cpq,qdcj->pdj", matrices.astype(jnp.float32), shaped)
    return parents.reshape(P_SIZE, devices * groups).astype(jnp.bfloat16)


def interact(matrices, table, codes, valid):
    width = NOFF // 4
    total = jnp.zeros((P_SIZE, codes.shape[1]), jnp.float32)
    for quarter in range(4):
        lower = quarter * width
        picked = jnp.take(table, codes[lower:lower + width], axis=1).astype(jnp.float32)
        picked = picked * valid[lower:lower + width].astype(jnp.float32)[None]
        total = total + jnp.einsum("opq,qot->pt", matrices[lower:lower + width], picked)
    return total


def ghost_table(multipoles, send_list, count, device):
    blocks = [lax.dynamic_slice_in_dim(multipoles, device * count, count, 1)]
    for bit_index in range(NBITS):
        partner = jnp.bitwise_xor(device, jnp.int32(1 << bit_index)).astype(jnp.int32)
        chosen = lax.dynamic_slice_in_dim(send_list, partner * count, count, 0)
        blocks.append(jnp.take(multipoles, (partner * count + chosen).astype(jnp.int32), axis=1))
    return jnp.concatenate(blocks, axis=1)


def level_pass(matrices, down_float, multipoles, send_list, codes, valid, coarser, count, factor):
    def one_device(device):
        table = ghost_table(multipoles, send_list, count, device)
        own_codes = lax.dynamic_slice_in_dim(codes, device * count, count, 1)
        own_valid = lax.dynamic_slice_in_dim(valid, device * count, count, 1)
        distant = factor * interact(matrices, table, own_codes, own_valid)
        above = lax.dynamic_slice_in_dim(coarser, device * (count // 8), count // 8, 1).astype(jnp.float32)
        inherited = jnp.einsum("cpq,qk->pck", down_float, above).reshape(P_SIZE, count)
        return distant + inherited
    result = lax.map(one_device, jnp.arange(N_GX * N_GY, dtype=jnp.int32))
    return jnp.transpose(result, (1, 0, 2)).reshape(P_SIZE, N_GX * N_GY * count)


def reference(leaf_multipole, up_matrices, down_matrices, far_matrices, send_leaf, send_parent, codes_leaf, valid_leaf, codes_parent, valid_parent, codes_coarse, valid_coarse):
    matrices = far_matrices.astype(jnp.float32)
    down_float = down_matrices.astype(jnp.float32)
    parent_mult = upward(up_matrices, leaf_multipole, PARENT_DEV)
    coarse_mult = upward(up_matrices, parent_mult, COARSE_DEV)
    coarse_local = interact(matrices, coarse_mult, codes_coarse, valid_coarse).astype(jnp.bfloat16)
    parent_local = level_pass(matrices, down_float, parent_mult, send_parent, codes_parent, valid_parent, coarse_local, PARENT_DEV, 2.0).astype(jnp.bfloat16)
    return level_pass(matrices, down_float, leaf_multipole, send_leaf, codes_leaf, valid_leaf, parent_local, LEAF_DEV, 4.0)
```

```python
import jax
import jax.numpy as jnp
from jax import lax
from jax.experimental import pallas as pl
from jax.experimental.pallas import tpu as pltpu
from jax.sharding import PartitionSpec as P

NOFF, P_SIZE = 316, 152
SUB = 4
BLOCK = 8
NSUB = 80
NBLOCK = NSUB * SUB // BLOCK
TARGETS, ROWS = 292, 296
TABLE = 2824

def main_kernel(codes_ref, w_ref, own_ref, g0, g1, g2, g3, g4, g5, g6, pown_ref, coarse_ref, down_ref, out_ref,
                table, wbuf, c0, c1, p0, p1, acc, wsem, csem):
    nit = NBLOCK // 2
    per = NSUB // nit
    codes = (c0, c1)
    picks = (p0, p1)
    def wcopy(i):
        return pltpu.make_async_copy(w_ref.at[pl.ds(i * per, per), pl.ds(0, P_SIZE)], wbuf.at[pl.ds(i * per, per)], wsem.at[i])
    def ccopy(b, slot):
        return pltpu.make_async_copy(codes_ref.at[b], codes[slot], csem.at[slot])
    ccopy(0, 0).start()
    ccopy(1, 1).start()
    for i in range(nit):
        wcopy(i).start()
    flat = table.reshape(TABLE * 2, 128)
    def fill(base, rows):
        n = rows.shape[0]
        wide = rows.astype(jnp.float32)
        flat[pl.ds(2 * base, n, stride=2), :] = wide[:, :128]
        flat[pl.ds(2 * base + 1, n, stride=2), :] = jnp.concatenate(
            [wide[:, 128:], jnp.zeros((n, 256 - P_SIZE), jnp.float32)], axis=1)
    fill(0, own_ref[...])
    fill(2048, pown_ref[...])
    for b, g in enumerate((g0, g1, g2, g3, g4, g5, g6)):
        fill(256 + 256 * b, g[0:256, :])
        fill(2080 + 32 * b, g[256:288, :])
    fill(2304, coarse_ref[...])
    flat[2 * 2816:2 * 2824, :] = jnp.zeros((16, 128), jnp.float32)
    acc[...] = jnp.zeros_like(acc)
    for p in picks:
        for o in range(SUB):
            p[o * ROWS + TARGETS:(o + 1) * ROWS] = jnp.zeros((ROWS - TARGETS, 2, 128), jnp.float32)

    def gather(slot, first, pick):
        for o in range(SUB):
            for t in range(TARGETS):
                word = (first + o) * 384 + t
                c = codes[slot][word // 128, word % 128]
                pick[o * ROWS + t] = flat[pl.ds(c, 2), :]
    def multiply(j, pick):
        lines = pick.reshape(SUB * ROWS * 2, 128)
        parts = []
        for o in range(SUB):
            for h in range(2):
                parts.append(lines[pl.ds(o * ROWS * 2 + h, ROWS, stride=2), :].astype(jnp.bfloat16))
        x = jnp.concatenate(parts, axis=1)
        acc[...] += lax.dot_general(x, wbuf[j], (((1,), (1,)), ((), ())), preferred_element_type=jnp.float32)

    def body(i, _):
        wcopy(i).wait()
        for slot in range(2):
            ccopy(2 * i + slot, slot).wait()
            for s in range(2):
                k = slot * 2 + s
                gather(slot, s * SUB, picks[s])
                multiply(4 * i + k, picks[s])
            @pl.when(i < nit - 1)
            def _():
                ccopy(2 * i + slot + 2, slot).start()
        return 0
    lax.fori_loop(0, nit, body, 0)

    nt = (((1,), (1,)), ((), ()))
    coarse_local = acc[288:296, :].astype(jnp.bfloat16)
    spread = [lax.dot_general(coarse_local, down_ref[c], nt, preferred_element_type=jnp.float32)[0:4] for c in range(8)]
    parent_local = (2.0 * acc[256:288, :] + jnp.concatenate(spread, axis=0)).astype(jnp.bfloat16)
    for c in range(8):
        inherited = lax.dot_general(parent_local, down_ref[c], nt, preferred_element_type=jnp.float32)
        acc[c * 32:(c + 1) * 32, :] = 4.0 * acc[c * 32:(c + 1) * 32, :] + inherited
    out_ref[...] = acc[0:256, :].T

def main_call(codes, w, own, ghosts, pown, coarse, down):
    vm = pl.BlockSpec(memory_space=pltpu.VMEM)
    anyspec = pl.BlockSpec(memory_space=pl.ANY)
    return pl.pallas_call(
        main_kernel,
        in_specs=[anyspec, anyspec] + [vm] * 11,
        out_specs=vm,
        out_shape=jax.ShapeDtypeStruct((P_SIZE, 256), jnp.float32),
        scratch_shapes=[
            pltpu.VMEM((TABLE, 2, 128), jnp.float32),
            pltpu.VMEM((NSUB, P_SIZE, SUB * 256), jnp.bfloat16),
            pltpu.SMEM((24, 128), jnp.int32), pltpu.SMEM((24, 128), jnp.int32),
            pltpu.VMEM((SUB * ROWS, 2, 128), jnp.float32), pltpu.VMEM((SUB * ROWS, 2, 128), jnp.float32),
            pltpu.VMEM((ROWS, P_SIZE), jnp.float32),
            pltpu.SemaphoreType.DMA((NBLOCK // 2,)), pltpu.SemaphoreType.DMA((2,)),
        ],
        compiler_params=pltpu.CompilerParams(vmem_limit_bytes=58 << 20),
        cost_estimate=pl.CostEstimate(flops=2 * 296 * 48032 * 152, bytes_accessed=28_000_000, transcendentals=0),
    )(codes, w, own, *ghosts, pown, coarse, down)

PBLOCK, STRIDE = 16, 328


def relay_kernel(f_ref, o_ref, low, high):
    for p in range(PBLOCK):
        wide = jnp.concatenate([f_ref[p].astype(jnp.float32), jnp.zeros((256 - P_SIZE, NOFF), jnp.float32)], axis=0)
        turned = wide.T
        low[p * STRIDE:p * STRIDE + NOFF, :] = turned[:, :128]
        high[p * STRIDE:p * STRIDE + NOFF, :] = turned[:, 128:]
    for o in range(NOFF):
        at = (o % SUB) * 256
        o_ref[o // SUB, :, at:at + 128] = low[pl.ds(o, PBLOCK, stride=STRIDE), :].astype(jnp.bfloat16)
        o_ref[o // SUB, :, at + 128:at + 256] = high[pl.ds(o, PBLOCK, stride=STRIDE), :].astype(jnp.bfloat16)
    o_ref[NOFF // SUB] = jnp.zeros((PBLOCK, SUB * 256), jnp.bfloat16)


def relay(far):
    return pl.pallas_call(
        relay_kernel,
        grid=(160 // PBLOCK,),
        in_specs=[pl.BlockSpec((PBLOCK, P_SIZE, NOFF), lambda i: (i, 0, 0))],
        out_specs=pl.BlockSpec((NSUB, PBLOCK, SUB * 256), lambda i: (0, i, 0)),
        out_shape=jax.ShapeDtypeStruct((NSUB, 160, SUB * 256), jnp.bfloat16),
        scratch_shapes=[pltpu.VMEM((STRIDE * PBLOCK, 128), jnp.float32)] * 2,
        compiler_params=pltpu.CompilerParams(vmem_limit_bytes=58 << 20),
        cost_estimate=pl.CostEstimate(flops=0, bytes_accessed=45_000_000, transcendentals=0),
    )(jnp.transpose(far, (1, 2, 0)))


def swapped(array, axis, distance):
    return lax.ppermute(array, axis, [(i, i ^ 1 << distance) for i in range(lax.axis_size(axis))])


def upward(matrices, children):
    groups = children.shape[1] // 8
    shaped = children.reshape(P_SIZE, 8, groups)
    return jnp.einsum("cpq,qcj->pj", matrices, shaped, preferred_element_type=jnp.float32).astype(jnp.bfloat16)


def listed(codes, valid, base):
    return jnp.where(valid > 0, 2 * (codes + base), 2 * 2816)


def shards(
    leaf_multipole,
    up_matrices,
    down_matrices,
    far_matrices,
    send_leaf,
    send_parent,
    codes_leaf,
    valid_leaf,
    codes_parent,
    valid_parent,
    codes_coarse,
    valid_coarse,
):
    own = leaf_multipole.T
    parent_mult = upward(up_matrices, leaf_multipole)
    parent_own = parent_mult.T
    coarse_mult = upward(up_matrices, parent_mult).T
    outgoing = jnp.concatenate(
        [
            own.at[send_leaf].get(mode="promise_in_bounds"),
            parent_own.at[send_parent].get(mode="promise_in_bounds"),
        ],
        axis=0,
    )
    ghosts = [swapped(outgoing, "gy", b) for b in range(5)] + [swapped(outgoing, "gx", b) for b in range(2)]
    spread = jnp.broadcast_to(coarse_mult[None], (128, 4, P_SIZE))
    coarse_all = lax.all_to_all(spread, ("gx", "gy"), 0, 0, tiled=True).reshape(512, P_SIZE)
    codes = jnp.concatenate(
        [
            listed(codes_leaf, valid_leaf, 0),
            listed(codes_parent, valid_parent, 2048),
            listed(codes_coarse, valid_coarse, 2304),
        ],
        axis=1,
    )
    codes = jnp.pad(codes, ((0, 4), (0, 384 - TARGETS)), constant_values=2 * 2816)
    codes = codes.reshape(NBLOCK, BLOCK * 3, 128)
    return main_call(codes, relay(far_matrices), own, ghosts, parent_own, coarse_all, down_matrices)


def solution(mesh):
    spec = P(None, ("gx", "gy"))
    flat = P(("gx", "gy"))
    return jax.shard_map(
        shards,
        mesh=mesh,
        in_specs=(spec, P(), P(), P(), flat, flat, spec, spec, spec, spec, spec, spec),
        out_specs=spec,
        check_vma=False,
    )
```

```python
import jax
import jax.numpy as jnp
from jax import lax
from jax.experimental import pallas as pl
from jax.experimental.pallas import tpu as pltpu
from jax.sharding import PartitionSpec as P

NOFF, P_SIZE = 316, 152
BLOCK = 8
COPIED = 5
NBLOCK = 40
LEAVES, PARENTS, COARSE = 256, 32, 4
ROWS = 296
TABLE, ZERO = 2568, 2560
PADDED = 160
PIECE = 512
NT = (((1,), (1,)), ((), ()))


def main_kernel(codes_ref, lanes_ref, plane_ref, w_ref, own_ref, g0, g1, g2, g3, g4, g5, g6, pown_ref, coarse_ref,
                down_ref, out_ref, table, columns, held, ptable, wbuf, c0, c1, p0, p1, acc, turned, wsem, csem):
    nit = NBLOCK // 2
    codes, picks = (c0, c1), (p0, p1)

    def wcopy(i):
        return pltpu.make_async_copy(w_ref.at[pl.ds(i * 2, 2)], wbuf.at[pl.ds(i * 2, 2)], wsem.at[i])

    def ccopy(b, slot):
        return pltpu.make_async_copy(codes_ref.at[b], codes[slot], csem.at[slot])

    ccopy(0, 0).start()
    ccopy(1, 1).start()
    for i in range(nit):
        wcopy(i).start()
    flat = table.reshape(TABLE * 2, 128)

    def widened(rows):
        wide = rows.astype(jnp.float32)
        return jnp.concatenate([wide, jnp.zeros((rows.shape[0], 256 - P_SIZE), jnp.float32)], axis=1)

    def fill(base, wide):
        n = wide.shape[0]
        flat[pl.ds(2 * base, n, stride=2), :] = wide[:, :128]
        flat[pl.ds(2 * base + 1, n, stride=2), :] = wide[:, 128:]

    held[...] = jnp.zeros_like(held)
    for b, g in enumerate((own_ref, g0, g1, g2, g3, g4, g5, g6)):
        wide = widened(g[0:LEAVES, :])
        fill(LEAVES * b, wide)
        columns[:, LEAVES * b:LEAVES * (b + 1)] = wide.T[0:PADDED].astype(jnp.bfloat16)
    fill(2048, widened(coarse_ref[...]))
    flat[2 * ZERO:2 * TABLE, :] = jnp.zeros((2 * (TABLE - ZERO), 128), jnp.float32)
    parents = jnp.concatenate([pown_ref[...].astype(jnp.float32)] + [g[LEAVES:LEAVES + PARENTS, :].astype(jnp.float32) for g in (g0, g1, g2, g3, g4, g5, g6)], axis=0)
    ptable[...] = widened(parents).T.astype(jnp.bfloat16)
    acc[...] = jnp.zeros_like(acc)
    turned[...] = jnp.zeros_like(turned)
    for p in picks:
        for o in range(BLOCK):
            at = COPIED * LEAVES + o * 8
            p[at + COARSE:at + 8] = jnp.zeros((8 - COARSE, 2, 128), jnp.float32)

    def copy_rows(slot, start, stop):
        for word in range(start, stop):
            picks[slot][word] = flat[pl.ds(codes[slot][word // 128, word % 128], 2), :]

    def chosen(column, depth, base):
        hot = lax.broadcasted_iota(jnp.int32, (depth, column.shape[1]), 0) == column - base
        return jnp.where(hot, 1.0, 0.0).astype(jnp.bfloat16)

    def block(b, slot):
        pieces = [(o, k) for o in range(BLOCK - COPIED) for k in range(2048 // PIECE)]
        share = COPIED * LEAVES // len(pieces)
        wide = jnp.dot(ptable[...], chosen(plane_ref[b], 256, 0), preferred_element_type=jnp.float32).T
        lines = picks[slot].reshape((COPIED * LEAVES + BLOCK * 8) * 2, 128)
        for o in range(BLOCK):
            for t in range(COARSE):
                pick_row = flat[pl.ds(codes[slot][(COPIED * LEAVES) // 128, o * COARSE + t], 2), :]
                picks[slot][COPIED * LEAVES + o * 8 + t] = pick_row
        for n, (o, k) in enumerate(pieces):
            @pl.when(b >= 0)
            def _():
                hot = chosen(lanes_ref[b, COPIED + o:COPIED + o + 1, :], PIECE, k * PIECE)
                found = jnp.dot(columns[:, k * PIECE:(k + 1) * PIECE], hot, preferred_element_type=jnp.float32)
                rows = slice(o * 256, o * 256 + PADDED)
                copy_rows(slot, n * share, COPIED * LEAVES if n == len(pieces) - 1 else (n + 1) * share)
                held[rows, :] = found if k == 0 else held[rows, :] + found

        def few(o, h):
            at = COPIED * LEAVES + o * 8
            return [wide[o * PARENTS:(o + 1) * PARENTS, h * 128:h * 128 + 128], lines[pl.ds(2 * at + h, 8, stride=2), :]]

        tail = wbuf[b, :, COPIED * 256:BLOCK * 256]
        turned[...] += jnp.dot(tail, held[...].astype(jnp.bfloat16), preferred_element_type=jnp.float32)
        rest = jnp.concatenate([jnp.concatenate(few(o, h), axis=0).astype(jnp.bfloat16) for o in range(COPIED, BLOCK) for h in range(2)], axis=1)
        acc[LEAVES:ROWS, :] += lax.dot_general(rest, tail, NT, preferred_element_type=jnp.float32)
        x = jnp.concatenate(
            [
                jnp.concatenate([lines[pl.ds(o * LEAVES * 2 + h, LEAVES, stride=2), :]] + few(o, h), axis=0).astype(jnp.bfloat16)
                for o in range(COPIED)
                for h in range(2)
            ],
            axis=1,
        )
        acc[...] += lax.dot_general(x, wbuf[b, :, 0:COPIED * 256], NT, preferred_element_type=jnp.float32)

    def body(i, _):
        wcopy(i).wait()
        for slot in range(2):
            ccopy(2 * i + slot, slot).wait()
            block(2 * i + slot, slot)
            @pl.when(i < nit - 1)
            def _():
                ccopy(2 * i + slot + 2, slot).start()
        return 0

    lax.fori_loop(0, nit, body, 0)

    coarse_local = acc[288:296, 0:P_SIZE].astype(jnp.bfloat16)
    spread = [lax.dot_general(coarse_local, down_ref[c], NT, preferred_element_type=jnp.float32)[0:4] for c in range(8)]
    parent_local = (2.0 * acc[256:288, 0:P_SIZE] + jnp.concatenate(spread, axis=0)).astype(jnp.bfloat16)
    inherited = [lax.dot_general(parent_local, down_ref[c], NT, preferred_element_type=jnp.float32) for c in range(8)]
    far = 4.0 * acc[0:256, 0:P_SIZE] + jnp.concatenate(inherited, axis=0)
    out_ref[...] = far.T + 4.0 * turned[0:P_SIZE, :]


def main_call(codes, lanes, plane, w, own, ghosts, pown, coarse, down):
    vm = pl.BlockSpec(memory_space=pltpu.VMEM)
    anyspec = pl.BlockSpec(memory_space=pl.ANY)
    picked = COPIED * LEAVES + BLOCK * 8
    return pl.pallas_call(
        main_kernel,
        in_specs=[anyspec, vm, vm, anyspec] + [vm] * 11,
        out_specs=vm,
        out_shape=jax.ShapeDtypeStruct((P_SIZE, LEAVES), jnp.float32),
        scratch_shapes=[
            pltpu.VMEM((TABLE, 2, 128), jnp.float32),
            pltpu.VMEM((PADDED, 2048), jnp.bfloat16),
            pltpu.VMEM(((BLOCK - COPIED) * 256, LEAVES), jnp.float32),
            pltpu.VMEM((256, 256), jnp.bfloat16),
            pltpu.VMEM((NBLOCK, PADDED, BLOCK * 256), jnp.bfloat16),
            pltpu.SMEM((16, 128), jnp.int32), pltpu.SMEM((16, 128), jnp.int32),
            pltpu.VMEM((picked, 2, 128), jnp.float32), pltpu.VMEM((picked, 2, 128), jnp.float32),
            pltpu.VMEM((ROWS, PADDED), jnp.float32),
            pltpu.VMEM((PADDED, LEAVES), jnp.float32),
            pltpu.SemaphoreType.DMA((NBLOCK // 2,)), pltpu.SemaphoreType.DMA((2,)),
        ],
        compiler_params=pltpu.CompilerParams(vmem_limit_bytes=58 << 20),
        cost_estimate=pl.CostEstimate(flops=2 * 296 * 48032 * 152, bytes_accessed=28_000_000, transcendentals=0),
    )(codes, lanes, plane, w, own, *ghosts, pown, coarse, down)


def tables(codes_leaf, valid_leaf, codes_parent, valid_parent, codes_coarse, valid_coarse):
    grow = ((0, BLOCK * NBLOCK - NOFF), (0, 0))
    lanes = jnp.pad(jnp.where(valid_leaf > 0, codes_leaf, -1), grow, constant_values=-1).reshape(NBLOCK, BLOCK, LEAVES)
    plane = jnp.pad(jnp.where(valid_parent > 0, codes_parent, -1), grow, constant_values=-1)
    plane = plane.reshape(NBLOCK, 1, BLOCK * PARENTS)
    coarse = jnp.pad(jnp.where(valid_coarse > 0, codes_coarse + 2048, ZERO), grow, constant_values=ZERO)
    coarse = jnp.pad(coarse.reshape(NBLOCK, 1, BLOCK * COARSE), ((0, 0), (0, 15 - 2 * COPIED), (0, 128 - BLOCK * COARSE)))
    rows = lanes[:, 0:COPIED].reshape(NBLOCK, COPIED * 2, 128)
    codes = 2 * jnp.concatenate([jnp.where(rows < 0, ZERO, rows), coarse], axis=1)
    return codes, lanes, plane

PBLOCK, STRIDE = 16, 328


def relay_kernel(f_ref, o_ref, low, high):
    for p in range(PBLOCK):
        wide = jnp.concatenate([f_ref[p].astype(jnp.float32), jnp.zeros((256 - P_SIZE, NOFF), jnp.float32)], axis=0)
        turned = wide.T
        low[p * STRIDE:p * STRIDE + NOFF, :] = turned[:, :128]
        high[p * STRIDE:p * STRIDE + NOFF, :] = turned[:, 128:]
    for o in range(NOFF):
        at = (o % BLOCK) * 256
        o_ref[o // BLOCK, :, at:at + 128] = low[pl.ds(o, PBLOCK, stride=STRIDE), :].astype(jnp.bfloat16)
        o_ref[o // BLOCK, :, at + 128:at + 256] = high[pl.ds(o, PBLOCK, stride=STRIDE), :].astype(jnp.bfloat16)
    o_ref[NBLOCK - 1, :, (NOFF % BLOCK) * 256:] = jnp.zeros((PBLOCK, (BLOCK - NOFF % BLOCK) * 256), jnp.bfloat16)


def relay(far):
    return pl.pallas_call(
        relay_kernel,
        grid=(PADDED // PBLOCK,),
        in_specs=[pl.BlockSpec((PBLOCK, P_SIZE, NOFF), lambda i: (i, 0, 0))],
        out_specs=pl.BlockSpec((NBLOCK, PBLOCK, BLOCK * 256), lambda i: (0, i, 0)),
        out_shape=jax.ShapeDtypeStruct((NBLOCK, PADDED, BLOCK * 256), jnp.bfloat16),
        scratch_shapes=[pltpu.VMEM((STRIDE * PBLOCK, 128), jnp.float32)] * 2,
        compiler_params=pltpu.CompilerParams(vmem_limit_bytes=58 << 20),
        cost_estimate=pl.CostEstimate(flops=0, bytes_accessed=45_000_000, transcendentals=0),
    )(jnp.transpose(far, (1, 2, 0)))


def swapped(array, axis, distance):
    return lax.ppermute(array, axis, [(i, i ^ 1 << distance) for i in range(lax.axis_size(axis))])


def upward(matrices, children):
    groups = children.shape[1] // 8
    shaped = children.reshape(P_SIZE, 8, groups)
    return jnp.einsum("cpq,qcj->pj", matrices, shaped, preferred_element_type=jnp.float32).astype(jnp.bfloat16)


def shards(
    leaf_multipole,
    up_matrices,
    down_matrices,
    far_matrices,
    send_leaf,
    send_parent,
    codes_leaf,
    valid_leaf,
    codes_parent,
    valid_parent,
    codes_coarse,
    valid_coarse,
):
    own = leaf_multipole.T
    parent_mult = upward(up_matrices, leaf_multipole)
    parent_own = parent_mult.T
    coarse_mult = upward(up_matrices, parent_mult).T
    outgoing = jnp.concatenate(
        [
            own.at[send_leaf].get(mode="promise_in_bounds"),
            parent_own.at[send_parent].get(mode="promise_in_bounds"),
        ],
        axis=0,
    )
    ghosts = [swapped(outgoing, "gy", b) for b in range(5)] + [swapped(outgoing, "gx", b) for b in range(2)]
    spread = jnp.broadcast_to(coarse_mult[None], (128, 4, P_SIZE))
    coarse_all = lax.all_to_all(spread, ("gx", "gy"), 0, 0, tiled=True).reshape(512, P_SIZE)
    codes, lanes, plane = tables(codes_leaf, valid_leaf, codes_parent, valid_parent, codes_coarse, valid_coarse)
    return main_call(codes, lanes, plane, relay(far_matrices), own, ghosts, parent_own, coarse_all, down_matrices)


def solution(mesh):
    spec = P(None, ("gx", "gy"))
    flat = P(("gx", "gy"))
    return jax.shard_map(
        shards,
        mesh=mesh,
        in_specs=(spec, P(), P(), P(), flat, flat, spec, spec, spec, spec, spec, spec),
        out_specs=spec,
        check_vma=False,
    )
```

```python
import jax
import jax.numpy as jnp
from jax import lax
from jax.experimental import pallas as pl
from jax.experimental.pallas import tpu as pltpu
from jax.sharding import PartitionSpec as P

NOFF, P_SIZE = 316, 152
BLOCK = 8
COPIED = 6
NBLOCK = 40
LEAVES, PARENTS, COARSE = 256, 32, 4
ROWS = 296
TABLE, ZERO = 2568, 2560
PADDED = 160
PIECE = 512
NT = (((1,), (1,)), ((), ()))


def main_kernel(codes_ref, lanes_ref, plane_ref, w_ref, own_ref, g0, g1, g2, g3, g4, g5, g6, pown_ref, coarse_ref,
                down_ref, out_ref, table, columns, h0, h1, v0, v1, ptable, wbuf, c0, c1, p0, p1, acc, turned, wsem, csem):
    nit = NBLOCK // 2
    codes, picks, helds, wides = (c0, c1), (p0, p1), (h0, h1), (v0, v1)

    def wcopy(i):
        return pltpu.make_async_copy(w_ref.at[pl.ds(i * 2, 2)], wbuf.at[pl.ds(i * 2, 2)], wsem.at[i])

    def ccopy(b, slot):
        return pltpu.make_async_copy(codes_ref.at[b], codes[slot], csem.at[slot])

    ccopy(0, 0).start()
    ccopy(1, 1).start()
    for i in range(nit):
        wcopy(i).start()
    flat = table.reshape(TABLE * 2, 128)

    def widened(rows):
        wide = rows.astype(jnp.float32)
        return jnp.concatenate([wide, jnp.zeros((rows.shape[0], 256 - P_SIZE), jnp.float32)], axis=1)

    def fill(base, wide):
        n = wide.shape[0]
        flat[pl.ds(2 * base, n, stride=2), :] = wide[:, :128]
        flat[pl.ds(2 * base + 1, n, stride=2), :] = wide[:, 128:]

    for ref in (h0, h1, p1, v1):
        ref[...] = jnp.zeros_like(ref)
    for b, g in enumerate((own_ref, g0, g1, g2, g3, g4, g5, g6)):
        wide = widened(g[0:LEAVES, :])
        fill(LEAVES * b, wide)
        columns[:, LEAVES * b:LEAVES * (b + 1)] = wide.T[0:PADDED].astype(jnp.bfloat16)
    fill(2048, widened(coarse_ref[...]))
    flat[2 * ZERO:2 * TABLE, :] = jnp.zeros((2 * (TABLE - ZERO), 128), jnp.float32)
    parents = jnp.concatenate([pown_ref[...].astype(jnp.float32)] + [g[LEAVES:LEAVES + PARENTS, :].astype(jnp.float32) for g in (g0, g1, g2, g3, g4, g5, g6)], axis=0)
    ptable[...] = widened(parents).T.astype(jnp.bfloat16)
    acc[...] = jnp.zeros_like(acc)
    turned[...] = jnp.zeros_like(turned)
    for p in picks:
        for o in range(BLOCK):
            at = COPIED * LEAVES + o * 8
            p[at + COARSE:at + 8] = jnp.zeros((8 - COARSE, 2, 128), jnp.float32)

    def copy_rows(slot, start, stop):
        for word in range(start, stop):
            picks[slot][word] = flat[pl.ds(codes[slot][word // 128, word % 128], 2), :]

    def chosen(column, depth, base):
        hot = lax.broadcasted_iota(jnp.int32, (depth, column.shape[1]), 0) == column - base
        return jnp.where(hot, 1.0, 0.0).astype(jnp.bfloat16)

    def few(slot, o, h):
        at = COPIED * LEAVES + o * 8
        lines = picks[slot].reshape((COPIED * LEAVES + BLOCK * 8) * 2, 128)
        return [wides[slot][o * PARENTS:(o + 1) * PARENTS, h * 128:h * 128 + 128], lines[pl.ds(2 * at + h, 8, stride=2), :]]

    def multiply(b, slot, o):
        if o < COPIED:
            lines = picks[slot].reshape((COPIED * LEAVES + BLOCK * 8) * 2, 128)
            x = [jnp.concatenate([lines[pl.ds(o * LEAVES * 2 + h, LEAVES, stride=2), :]] + few(slot, o, h), axis=0).astype(jnp.bfloat16) for h in range(2)]
            acc[...] += lax.dot_general(jnp.concatenate(x, axis=1), wbuf[b, :, o * 256:(o + 1) * 256], NT, preferred_element_type=jnp.float32)
        elif o == COPIED:
            turned[...] += jnp.dot(wbuf[b, :, COPIED * 256:BLOCK * 256], helds[slot][...].astype(jnp.bfloat16), preferred_element_type=jnp.float32)
        else:
            x = [jnp.concatenate(few(slot, o, h), axis=0).astype(jnp.bfloat16) for o in range(COPIED, BLOCK) for h in range(2)]
            acc[LEAVES:ROWS, :] += lax.dot_general(jnp.concatenate(x, axis=1), wbuf[b, :, COPIED * 256:BLOCK * 256], NT, preferred_element_type=jnp.float32)

    pieces = [(o, k) for o in range(BLOCK - COPIED) for k in range(2048 // PIECE)]
    share = COPIED * LEAVES // len(pieces)

    def block(b, slot):
        for n, (o, k) in enumerate(pieces):
            @pl.when(b >= 0)
            def _():
                hot = chosen(lanes_ref[b, COPIED + o:COPIED + o + 1, :], PIECE, k * PIECE)
                found = jnp.dot(columns[:, k * PIECE:(k + 1) * PIECE], hot, preferred_element_type=jnp.float32)
                if n < COPIED + 2:
                    multiply(jnp.maximum(b - 1, 0), 1 - slot, n)
                copy_rows(slot, n * share, COPIED * LEAVES if n == len(pieces) - 1 else (n + 1) * share)
                rows = slice(o * 256, o * 256 + PADDED)
                helds[slot][rows, :] = found if k == 0 else helds[slot][rows, :] + found
                if n == len(pieces) - 1:
                    wides[slot][...] = jnp.dot(ptable[...], chosen(plane_ref[b], 256, 0), preferred_element_type=jnp.float32).T
                    for m in range(BLOCK):
                        for t in range(COARSE):
                            code = codes[slot][(COPIED * LEAVES) // 128, m * COARSE + t]
                            picks[slot][COPIED * LEAVES + m * 8 + t] = flat[pl.ds(code, 2), :]

    def body(i, _):
        wcopy(i).wait()
        for slot in range(2):
            ccopy(2 * i + slot, slot).wait()
            block(2 * i + slot, slot)
            @pl.when(i < nit - 1)
            def _():
                ccopy(2 * i + slot + 2, slot).start()
        return 0

    lax.fori_loop(0, nit, body, 0)
    for n in range(COPIED + 2):
        multiply(NBLOCK - 1, 1, n)

    coarse_local = acc[288:296, 0:P_SIZE].astype(jnp.bfloat16)
    spread = [lax.dot_general(coarse_local, down_ref[c], NT, preferred_element_type=jnp.float32)[0:4] for c in range(8)]
    parent_local = (2.0 * acc[256:288, 0:P_SIZE] + jnp.concatenate(spread, axis=0)).astype(jnp.bfloat16)
    inherited = [lax.dot_general(parent_local, down_ref[c], NT, preferred_element_type=jnp.float32) for c in range(8)]
    far = 4.0 * acc[0:256, 0:P_SIZE] + jnp.concatenate(inherited, axis=0)
    out_ref[...] = far.T + 4.0 * turned[0:P_SIZE, :]


def main_call(codes, lanes, plane, w, own, ghosts, pown, coarse, down):
    vm = pl.BlockSpec(memory_space=pltpu.VMEM)
    anyspec = pl.BlockSpec(memory_space=pl.ANY)
    picked = COPIED * LEAVES + BLOCK * 8
    return pl.pallas_call(
        main_kernel,
        in_specs=[anyspec, vm, vm, anyspec] + [vm] * 11,
        out_specs=vm,
        out_shape=jax.ShapeDtypeStruct((P_SIZE, LEAVES), jnp.float32),
        scratch_shapes=[
            pltpu.VMEM((TABLE, 2, 128), jnp.float32),
            pltpu.VMEM((PADDED, 2048), jnp.bfloat16),
            pltpu.VMEM(((BLOCK - COPIED) * 256, LEAVES), jnp.float32), pltpu.VMEM(((BLOCK - COPIED) * 256, LEAVES), jnp.float32),
            pltpu.VMEM((256, 256), jnp.float32), pltpu.VMEM((256, 256), jnp.float32),
            pltpu.VMEM((256, 256), jnp.bfloat16),
            pltpu.VMEM((NBLOCK, PADDED, BLOCK * 256), jnp.bfloat16),
            pltpu.SMEM((16, 128), jnp.int32), pltpu.SMEM((16, 128), jnp.int32),
            pltpu.VMEM((picked, 2, 128), jnp.float32), pltpu.VMEM((picked, 2, 128), jnp.float32),
            pltpu.VMEM((ROWS, PADDED), jnp.float32),
            pltpu.VMEM((PADDED, LEAVES), jnp.float32),
            pltpu.SemaphoreType.DMA((NBLOCK // 2,)), pltpu.SemaphoreType.DMA((2,)),
        ],
        compiler_params=pltpu.CompilerParams(vmem_limit_bytes=58 << 20),
        cost_estimate=pl.CostEstimate(flops=2 * 296 * 48032 * 152, bytes_accessed=28_000_000, transcendentals=0),
    )(codes, lanes, plane, w, own, *ghosts, pown, coarse, down)


def tables(codes_leaf, valid_leaf, codes_parent, valid_parent, codes_coarse, valid_coarse):
    grow = ((0, BLOCK * NBLOCK - NOFF), (0, 0))
    lanes = jnp.pad(jnp.where(valid_leaf > 0, codes_leaf, -1), grow, constant_values=-1).reshape(NBLOCK, BLOCK, LEAVES)
    plane = jnp.pad(jnp.where(valid_parent > 0, codes_parent, -1), grow, constant_values=-1)
    plane = plane.reshape(NBLOCK, 1, BLOCK * PARENTS)
    coarse = jnp.pad(jnp.where(valid_coarse > 0, codes_coarse + 2048, ZERO), grow, constant_values=ZERO)
    coarse = jnp.pad(coarse.reshape(NBLOCK, 1, BLOCK * COARSE), ((0, 0), (0, 15 - 2 * COPIED), (0, 128 - BLOCK * COARSE)))
    rows = lanes[:, 0:COPIED].reshape(NBLOCK, COPIED * 2, 128)
    codes = 2 * jnp.concatenate([jnp.where(rows < 0, ZERO, rows), coarse], axis=1)
    return codes, lanes, plane

PBLOCK, STRIDE = 16, 328


def relay_kernel(f_ref, o_ref, low, high):
    for p in range(PBLOCK):
        wide = jnp.concatenate([f_ref[p].astype(jnp.float32), jnp.zeros((256 - P_SIZE, NOFF), jnp.float32)], axis=0)
        turned = wide.T
        low[p * STRIDE:p * STRIDE + NOFF, :] = turned[:, :128]
        high[p * STRIDE:p * STRIDE + NOFF, :] = turned[:, 128:]
    for o in range(NOFF):
        at = (o % BLOCK) * 256
        o_ref[o // BLOCK, :, at:at + 128] = low[pl.ds(o, PBLOCK, stride=STRIDE), :].astype(jnp.bfloat16)
        o_ref[o // BLOCK, :, at + 128:at + 256] = high[pl.ds(o, PBLOCK, stride=STRIDE), :].astype(jnp.bfloat16)
    o_ref[NBLOCK - 1, :, (NOFF % BLOCK) * 256:] = jnp.zeros((PBLOCK, (BLOCK - NOFF % BLOCK) * 256), jnp.bfloat16)


def relay(far):
    return pl.pallas_call(
        relay_kernel,
        grid=(PADDED // PBLOCK,),
        in_specs=[pl.BlockSpec((PBLOCK, P_SIZE, NOFF), lambda i: (i, 0, 0))],
        out_specs=pl.BlockSpec((NBLOCK, PBLOCK, BLOCK * 256), lambda i: (0, i, 0)),
        out_shape=jax.ShapeDtypeStruct((NBLOCK, PADDED, BLOCK * 256), jnp.bfloat16),
        scratch_shapes=[pltpu.VMEM((STRIDE * PBLOCK, 128), jnp.float32)] * 2,
        compiler_params=pltpu.CompilerParams(vmem_limit_bytes=58 << 20),
        cost_estimate=pl.CostEstimate(flops=0, bytes_accessed=45_000_000, transcendentals=0),
    )(jnp.transpose(far, (1, 2, 0)))


def swapped(array, axis, distance):
    return lax.ppermute(array, axis, [(i, i ^ 1 << distance) for i in range(lax.axis_size(axis))])


def upward(matrices, children):
    groups = children.shape[1] // 8
    shaped = children.reshape(P_SIZE, 8, groups)
    return jnp.einsum("cpq,qcj->pj", matrices, shaped, preferred_element_type=jnp.float32).astype(jnp.bfloat16)


def shards(
    leaf_multipole,
    up_matrices,
    down_matrices,
    far_matrices,
    send_leaf,
    send_parent,
    codes_leaf,
    valid_leaf,
    codes_parent,
    valid_parent,
    codes_coarse,
    valid_coarse,
):
    own = leaf_multipole.T
    parent_mult = upward(up_matrices, leaf_multipole)
    parent_own = parent_mult.T
    coarse_mult = upward(up_matrices, parent_mult).T
    outgoing = jnp.concatenate(
        [
            own.at[send_leaf].get(mode="promise_in_bounds"),
            parent_own.at[send_parent].get(mode="promise_in_bounds"),
        ],
        axis=0,
    )
    ghosts = [swapped(outgoing, "gy", b) for b in range(5)] + [swapped(outgoing, "gx", b) for b in range(2)]
    spread = jnp.broadcast_to(coarse_mult[None], (128, 4, P_SIZE))
    coarse_all = lax.all_to_all(spread, ("gx", "gy"), 0, 0, tiled=True).reshape(512, P_SIZE)
    codes, lanes, plane = tables(codes_leaf, valid_leaf, codes_parent, valid_parent, codes_coarse, valid_coarse)
    return main_call(codes, lanes, plane, relay(far_matrices), own, ghosts, parent_own, coarse_all, down_matrices)


def solution(mesh):
    spec = P(None, ("gx", "gy"))
    flat = P(("gx", "gy"))
    return jax.shard_map(
        shards,
        mesh=mesh,
        in_specs=(spec, P(), P(), P(), flat, flat, spec, spec, spec, spec, spec, spec),
        out_specs=spec,
        check_vma=False,
    )
```

```python
import jax
import jax.numpy as jnp
from jax import lax
from jax.experimental import pallas as pl
from jax.experimental.pallas import tpu as pltpu
from jax.sharding import PartitionSpec as P

NOFF, P_SIZE = 316, 152
BLOCK = 8
COPIED = 6
NBLOCK = 40
LEAVES, PARENTS, COARSE = 256, 32, 4
ROWS = 296
TABLE, ZERO = 2568, 2560
PADDED, SPLIT = 160, 64
PIECE = 512
NT = (((1,), (1,)), ((), ()))


def main_kernel(codes_ref, lanes_ref, plane_ref, wa_ref, wb_ref, own_ref, g0, g1, g2, g3, g4, g5, g6, pown_ref, coarse_ref,
                down_ref, out_ref, table, columns, h0, h1, v0, v1, ptable, wbuf, c0, c1, p0, p1, acc, turned, wsem, csem):
    nit = NBLOCK // 2
    codes, picks, helds, wides = (c0, c1), (p0, p1), (h0, h1), (v0, v1)

    def wcopy(i, ref, half, first, last):
        to = wbuf.at[pl.ds(i * 2, 2), pl.ds(first, last - first)]
        return pltpu.make_async_copy(ref.at[pl.ds(i * 2, 2)], to, wsem.at[half, i])

    parts = ((wa_ref, 0, 0, SPLIT), (wb_ref, 1, SPLIT, PADDED))

    def ccopy(b, slot):
        return pltpu.make_async_copy(codes_ref.at[b], codes[slot], csem.at[slot])

    ccopy(0, 0).start()
    ccopy(1, 1).start()
    for i in range(nit):
        for part in parts:
            wcopy(i, *part).start()
    flat = table.reshape(TABLE * 2, 128)

    def widened(rows):
        wide = rows.astype(jnp.float32)
        return jnp.concatenate([wide, jnp.zeros((rows.shape[0], 256 - P_SIZE), jnp.float32)], axis=1)

    def fill(base, wide):
        n = wide.shape[0]
        flat[pl.ds(2 * base, n, stride=2), :] = wide[:, :128]
        flat[pl.ds(2 * base + 1, n, stride=2), :] = wide[:, 128:]

    for ref in (h0, h1, p1.reshape((COPIED * LEAVES + BLOCK * 8) * 2, 128), v1):
        ref[...] = jnp.zeros(ref.shape, jnp.float32)
    for b, g in enumerate((own_ref, g0, g1, g2, g3, g4, g5, g6)):
        wide = widened(g[0:LEAVES, :])
        fill(LEAVES * b, wide)
        columns[:, LEAVES * b:LEAVES * (b + 1)] = wide.T[0:PADDED].astype(jnp.bfloat16)
    fill(2048, widened(coarse_ref[...]))
    flat[2 * ZERO:2 * TABLE, :] = jnp.zeros((2 * (TABLE - ZERO), 128), jnp.float32)
    parents = jnp.concatenate([pown_ref[...].astype(jnp.float32)] + [g[LEAVES:LEAVES + PARENTS, :].astype(jnp.float32) for g in (g0, g1, g2, g3, g4, g5, g6)], axis=0)
    ptable[...] = widened(parents).T.astype(jnp.bfloat16)
    acc[...] = jnp.zeros_like(acc)
    turned[...] = jnp.zeros_like(turned)
    for p in picks:
        for o in range(BLOCK):
            at = COPIED * LEAVES + o * 8
            p[at + COARSE:at + 8] = jnp.zeros((8 - COARSE, 2, 128), jnp.float32)

    def copy_rows(slot, start, stop):
        for word in range(start, stop):
            picks[slot][word] = flat[pl.ds(codes[slot][word // 128, word % 128], 2), :]

    def chosen(column, depth, base):
        hot = lax.broadcasted_iota(jnp.int32, (depth, column.shape[1]), 0) == column - base
        return jnp.where(hot, 1.0, 0.0).astype(jnp.bfloat16)

    def few(slot, o, h):
        at = COPIED * LEAVES + o * 8
        lines = picks[slot].reshape((COPIED * LEAVES + BLOCK * 8) * 2, 128)
        return [wides[slot][o * PARENTS:(o + 1) * PARENTS, h * 128:h * 128 + 128], lines[pl.ds(2 * at + h, 8, stride=2), :]]

    def multiply(b, slot, o):
        if o < COPIED:
            lines = picks[slot].reshape((COPIED * LEAVES + BLOCK * 8) * 2, 128)
            x = [jnp.concatenate([lines[pl.ds(o * LEAVES * 2 + h, LEAVES, stride=2), :]] + few(slot, o, h), axis=0).astype(jnp.bfloat16) for h in range(2)]
            acc[...] += lax.dot_general(jnp.concatenate(x, axis=1), wbuf[b, :, o * 256:(o + 1) * 256], NT, preferred_element_type=jnp.float32)
        elif o == COPIED:
            turned[...] += jnp.dot(wbuf[b, :, COPIED * 256:BLOCK * 256], helds[slot][...].astype(jnp.bfloat16), preferred_element_type=jnp.float32)
        else:
            x = [jnp.concatenate(few(slot, o, h), axis=0).astype(jnp.bfloat16) for o in range(COPIED, BLOCK) for h in range(2)]
            acc[LEAVES:ROWS, :] += lax.dot_general(jnp.concatenate(x, axis=1), wbuf[b, :, COPIED * 256:BLOCK * 256], NT, preferred_element_type=jnp.float32)

    pieces = [(o, k) for o in range(BLOCK - COPIED) for k in range(2048 // PIECE)]
    share = COPIED * LEAVES // len(pieces)

    def block(b, slot):
        for n, (o, k) in enumerate(pieces):
            @pl.when(b >= 0)
            def _():
                hot = chosen(lanes_ref[b, COPIED + o:COPIED + o + 1, :], PIECE, k * PIECE)
                found = jnp.dot(columns[:, k * PIECE:(k + 1) * PIECE], hot, preferred_element_type=jnp.float32)
                if n < COPIED + 2:
                    multiply(jnp.maximum(b - 1, 0), 1 - slot, n)
                copy_rows(slot, n * share, COPIED * LEAVES if n == len(pieces) - 1 else (n + 1) * share)
                rows = slice(o * 256, o * 256 + PADDED)
                helds[slot][rows, :] = found if k == 0 else helds[slot][rows, :] + found
                if n == len(pieces) - 1:
                    wides[slot][...] = jnp.dot(ptable[...], chosen(plane_ref[b], 256, 0), preferred_element_type=jnp.float32).T
                    for m in range(BLOCK):
                        for t in range(COARSE):
                            code = codes[slot][(COPIED * LEAVES) // 128, m * COARSE + t]
                            picks[slot][COPIED * LEAVES + m * 8 + t] = flat[pl.ds(code, 2), :]

    def body(i, _):
        for part in parts:
            wcopy(i, *part).wait()
        for slot in range(2):
            ccopy(2 * i + slot, slot).wait()
            block(2 * i + slot, slot)
            @pl.when(i < nit - 1)
            def _():
                ccopy(2 * i + slot + 2, slot).start()
        return 0

    lax.fori_loop(0, nit, body, 0)
    for n in range(COPIED + 2):
        multiply(NBLOCK - 1, 1, n)

    coarse_local = acc[288:296, 0:P_SIZE].astype(jnp.bfloat16)
    spread = [lax.dot_general(coarse_local, down_ref[c], NT, preferred_element_type=jnp.float32)[0:4] for c in range(8)]
    parent_local = (2.0 * acc[256:288, 0:P_SIZE] + jnp.concatenate(spread, axis=0)).astype(jnp.bfloat16)
    inherited = [lax.dot_general(parent_local, down_ref[c], NT, preferred_element_type=jnp.float32) for c in range(8)]
    far = 4.0 * acc[0:256, 0:P_SIZE] + jnp.concatenate(inherited, axis=0)
    out_ref[...] = far.T + 4.0 * turned[0:P_SIZE, :]


def main_call(codes, lanes, plane, wa, wb, own, ghosts, pown, coarse, down):
    vm = pl.BlockSpec(memory_space=pltpu.VMEM)
    anyspec = pl.BlockSpec(memory_space=pl.ANY)
    picked = COPIED * LEAVES + BLOCK * 8
    return pl.pallas_call(
        main_kernel,
        in_specs=[anyspec, vm, vm, anyspec, anyspec] + [vm] * 11,
        out_specs=vm,
        out_shape=jax.ShapeDtypeStruct((P_SIZE, LEAVES), jnp.float32),
        scratch_shapes=[
            pltpu.VMEM((TABLE, 2, 128), jnp.float32),
            pltpu.VMEM((PADDED, 2048), jnp.bfloat16),
            pltpu.VMEM(((BLOCK - COPIED) * 256, LEAVES), jnp.float32), pltpu.VMEM(((BLOCK - COPIED) * 256, LEAVES), jnp.float32),
            pltpu.VMEM((256, 256), jnp.float32), pltpu.VMEM((256, 256), jnp.float32),
            pltpu.VMEM((256, 256), jnp.bfloat16),
            pltpu.VMEM((NBLOCK, PADDED, BLOCK * 256), jnp.bfloat16),
            pltpu.SMEM((16, 128), jnp.int32), pltpu.SMEM((16, 128), jnp.int32),
            pltpu.VMEM((picked, 2, 128), jnp.float32), pltpu.VMEM((picked, 2, 128), jnp.float32),
            pltpu.VMEM((ROWS, PADDED), jnp.float32),
            pltpu.VMEM((PADDED, LEAVES), jnp.float32),
            pltpu.SemaphoreType.DMA((2, NBLOCK // 2)), pltpu.SemaphoreType.DMA((2,)),
        ],
        compiler_params=pltpu.CompilerParams(vmem_limit_bytes=58 << 20),
        cost_estimate=pl.CostEstimate(flops=2 * 296 * 48032 * 152, bytes_accessed=28_000_000, transcendentals=0),
    )(codes, lanes, plane, wa, wb, own, *ghosts, pown, coarse, down)


def tables(codes_leaf, valid_leaf, codes_parent, valid_parent, codes_coarse, valid_coarse):
    grow = ((0, BLOCK * NBLOCK - NOFF), (0, 0))
    lanes = jnp.pad(jnp.where(valid_leaf > 0, codes_leaf, -1), grow, constant_values=-1).reshape(NBLOCK, BLOCK, LEAVES)
    plane = jnp.pad(jnp.where(valid_parent > 0, codes_parent, -1), grow, constant_values=-1)
    plane = plane.reshape(NBLOCK, 1, BLOCK * PARENTS)
    coarse = jnp.pad(jnp.where(valid_coarse > 0, codes_coarse + 2048, ZERO), grow, constant_values=ZERO)
    coarse = jnp.pad(coarse.reshape(NBLOCK, 1, BLOCK * COARSE), ((0, 0), (0, 15 - 2 * COPIED), (0, 128 - BLOCK * COARSE)))
    rows = lanes[:, 0:COPIED].reshape(NBLOCK, COPIED * 2, 128)
    codes = 2 * jnp.concatenate([jnp.where(rows < 0, ZERO, rows), coarse], axis=1)
    return codes, lanes, plane


PBLOCK, STRIDE = 32, 136


def relay_kernel(f_ref, *refs):
    o_ref, halves = refs[-7], refs[-6:]

    def turn(k, p):
        first, last = k * 128, min(k * 128 + 128, NOFF)
        wide = f_ref[p, :, first:last].astype(jnp.float32)
        wide = jnp.concatenate([wide, jnp.zeros((256 - P_SIZE, last - first), jnp.float32)], axis=0).T
        for h in range(2):
            halves[2 * k + h][p * STRIDE:p * STRIDE + last - first, :] = wide[:, h * 128:h * 128 + 128]

    def give(o):
        for h in range(2):
            lane = (o % BLOCK) * 256 + h * 128
            rows = halves[2 * (o // 128) + h][pl.ds(o % 128, PBLOCK, stride=STRIDE), :]
            o_ref[o // BLOCK, :, lane:lane + 128] = rows.astype(jnp.bfloat16)

    always = pl.program_id(0) >= 0
    for k in range(4):
        for quarter in range(4):
            @pl.when(always)
            def _():
                if k < 3:
                    for p in range(quarter * PBLOCK // 4, (quarter + 1) * PBLOCK // 4):
                        turn(k, p)
                if k > 0:
                    for o in range((k - 1) * 128 + quarter * 32, min((k - 1) * 128 + quarter * 32 + 32, NOFF)):
                        give(o)
    o_ref[NBLOCK - 1, :, (NOFF % BLOCK) * 256:] = jnp.zeros((PBLOCK, (BLOCK - NOFF % BLOCK) * 256), jnp.bfloat16)


def relay(far, first, last, after):
    start, steps = first // PBLOCK, (last - first) // PBLOCK
    return pl.pallas_call(
        relay_kernel,
        grid=(steps,),
        in_specs=[pl.BlockSpec((PBLOCK, P_SIZE, NOFF), lambda i: (i + start, 0, 0))] + [pl.BlockSpec(memory_space=pl.ANY)] * len(after),
        out_specs=pl.BlockSpec((NBLOCK, PBLOCK, BLOCK * 256), lambda i: (0, i, 0)),
        out_shape=jax.ShapeDtypeStruct((NBLOCK, last - first, BLOCK * 256), jnp.bfloat16),
        scratch_shapes=[pltpu.VMEM((STRIDE * PBLOCK, 128), jnp.float32)] * 6,
        compiler_params=pltpu.CompilerParams(vmem_limit_bytes=58 << 20),
        cost_estimate=pl.CostEstimate(flops=0, bytes_accessed=9_000_000 * steps, transcendentals=0),
    )(jnp.transpose(far, (1, 2, 0)), *after)


def swapped(array, axis, distance):
    return lax.ppermute(array, axis, [(i, i ^ 1 << distance) for i in range(lax.axis_size(axis))])


def upward(matrices, children):
    groups = children.shape[1] // 8
    shaped = children.reshape(P_SIZE, 8, groups)
    return jnp.einsum("cpq,qcj->pj", matrices, shaped, preferred_element_type=jnp.float32).astype(jnp.bfloat16)


def shards(
    leaf_multipole,
    up_matrices,
    down_matrices,
    far_matrices,
    send_leaf,
    send_parent,
    codes_leaf,
    valid_leaf,
    codes_parent,
    valid_parent,
    codes_coarse,
    valid_coarse,
):
    own = leaf_multipole.T
    parent_mult = upward(up_matrices, leaf_multipole)
    parent_own = parent_mult.T
    coarse_mult = upward(up_matrices, parent_mult).T
    outgoing = jnp.concatenate(
        [
            own.at[send_leaf].get(mode="promise_in_bounds"),
            parent_own.at[send_parent].get(mode="promise_in_bounds"),
        ],
        axis=0,
    )
    ghosts = [swapped(outgoing, "gy", b) for b in range(5)] + [swapped(outgoing, "gx", b) for b in range(2)]
    spread = jnp.broadcast_to(coarse_mult[None], (128, 4, P_SIZE))
    coarse_all = lax.all_to_all(spread, ("gx", "gy"), 0, 0, tiled=True).reshape(512, P_SIZE)
    first = relay(far_matrices, 0, SPLIT, [])
    second = relay(far_matrices, SPLIT, PADDED, ghosts[5:7])
    codes, lanes, plane = tables(codes_leaf, valid_leaf, codes_parent, valid_parent, codes_coarse, valid_coarse)
    return main_call(codes, lanes, plane, first, second, own, ghosts, parent_own, coarse_all, down_matrices)


def solution(mesh):
    spec = P(None, ("gx", "gy"))
    flat = P(("gx", "gy"))
    return jax.shard_map(
        shards,
        mesh=mesh,
        in_specs=(spec, P(), P(), P(), flat, flat, spec, spec, spec, spec, spec, spec),
        out_specs=spec,
        check_vma=False,
    )
```

```python
import jax
import jax.numpy as jnp
from jax import lax
from jax.experimental import pallas as pl
from jax.experimental.pallas import tpu as pltpu
from jax.sharding import PartitionSpec as P

NOFF, P_SIZE = 316, 152
BLOCK = 8
COPIED = 6
NBLOCK = 40
LEAVES, PARENTS, COARSE = 256, 32, 4
ROWS = 296
TABLE, ZERO = 2568, 2560
PADDED = 160
PIECE = 512
NT = (((1,), (1,)), ((), ()))


def main_kernel(codes_ref, lanes_ref, plane_ref, w_ref, own_ref, g0, g1, g2, g3, g4, g5, g6, pown_ref, coarse_ref,
                down_ref, out_ref, table, columns, h0, h1, v0, v1, ptable, wbuf, c0, c1, p0, p1, acc, turned, wsem, csem):
    nit = NBLOCK // 2
    codes, picks, helds, wides = (c0, c1), (p0, p1), (h0, h1), (v0, v1)

    def wcopy(i):
        return pltpu.make_async_copy(w_ref.at[pl.ds(i * 2, 2)], wbuf.at[pl.ds(i * 2, 2)], wsem.at[i])

    def ccopy(b, slot):
        return pltpu.make_async_copy(codes_ref.at[b], codes[slot], csem.at[slot])

    ccopy(0, 0).start()
    ccopy(1, 1).start()
    for i in range(nit):
        wcopy(i).start()
    flat = table.reshape(TABLE * 2, 128)

    def widened(rows):
        wide = rows.astype(jnp.float32)
        return jnp.concatenate([wide, jnp.zeros((rows.shape[0], 256 - P_SIZE), jnp.float32)], axis=1)

    def fill(base, wide):
        n = wide.shape[0]
        flat[pl.ds(2 * base, n, stride=2), :] = wide[:, :128]
        flat[pl.ds(2 * base + 1, n, stride=2), :] = wide[:, 128:]

    for ref in (h0, h1, p1.reshape((COPIED * LEAVES + BLOCK * 8) * 2, 128), v1):
        ref[...] = jnp.zeros(ref.shape, jnp.float32)
    for b, g in enumerate((own_ref, g0, g1, g2, g3, g4, g5, g6)):
        wide = widened(g[0:LEAVES, :])
        fill(LEAVES * b, wide)
        columns[:, LEAVES * b:LEAVES * (b + 1)] = wide.T[0:PADDED].astype(jnp.bfloat16)
    fill(2048, widened(coarse_ref[...]))
    flat[2 * ZERO:2 * TABLE, :] = jnp.zeros((2 * (TABLE - ZERO), 128), jnp.float32)
    parents = jnp.concatenate([pown_ref[...].astype(jnp.float32)] + [g[LEAVES:LEAVES + PARENTS, :].astype(jnp.float32) for g in (g0, g1, g2, g3, g4, g5, g6)], axis=0)
    ptable[...] = widened(parents).T.astype(jnp.bfloat16)
    acc[...] = jnp.zeros_like(acc)
    turned[...] = jnp.zeros_like(turned)
    for p in picks:
        for o in range(BLOCK):
            at = COPIED * LEAVES + o * 8
            p[at + COARSE:at + 8] = jnp.zeros((8 - COARSE, 2, 128), jnp.float32)

    def copy_rows(slot, start, stop):
        for word in range(start, stop):
            picks[slot][word] = flat[pl.ds(codes[slot][word // 128, word % 128], 2), :]

    def chosen(column, depth, base):
        hot = lax.broadcasted_iota(jnp.int32, (depth, column.shape[1]), 0) == column - base
        return jnp.where(hot, 1.0, 0.0).astype(jnp.bfloat16)

    def few(slot, o, h):
        at = COPIED * LEAVES + o * 8
        lines = picks[slot].reshape((COPIED * LEAVES + BLOCK * 8) * 2, 128)
        return [wides[slot][o * PARENTS:(o + 1) * PARENTS, h * 128:h * 128 + 128], lines[pl.ds(2 * at + h, 8, stride=2), :]]

    def multiply(b, slot, o):
        if o < COPIED:
            lines = picks[slot].reshape((COPIED * LEAVES + BLOCK * 8) * 2, 128)
            x = [jnp.concatenate([lines[pl.ds(o * LEAVES * 2 + h, LEAVES, stride=2), :]] + few(slot, o, h), axis=0).astype(jnp.bfloat16) for h in range(2)]
            acc[...] += lax.dot_general(jnp.concatenate(x, axis=1), wbuf[b, :, o * 256:(o + 1) * 256], NT, preferred_element_type=jnp.float32)
        elif o == COPIED:
            turned[...] += jnp.dot(wbuf[b, :, COPIED * 256:BLOCK * 256], helds[slot][...].astype(jnp.bfloat16), preferred_element_type=jnp.float32)
        else:
            x = [jnp.concatenate(few(slot, o, h), axis=0).astype(jnp.bfloat16) for o in range(COPIED, BLOCK) for h in range(2)]
            acc[LEAVES:ROWS, :] += lax.dot_general(jnp.concatenate(x, axis=1), wbuf[b, :, COPIED * 256:BLOCK * 256], NT, preferred_element_type=jnp.float32)

    pieces = [(o, k) for o in range(BLOCK - COPIED) for k in range(2048 // PIECE)]
    share = COPIED * LEAVES // len(pieces)

    def block(b, slot):
        for n, (o, k) in enumerate(pieces):
            @pl.when(b >= 0)
            def _():
                hot = chosen(lanes_ref[b, COPIED + o:COPIED + o + 1, :], PIECE, k * PIECE)
                found = jnp.dot(columns[:, k * PIECE:(k + 1) * PIECE], hot, preferred_element_type=jnp.float32)
                if n < COPIED + 2:
                    multiply(jnp.maximum(b - 1, 0), 1 - slot, n)
                copy_rows(slot, n * share, COPIED * LEAVES if n == len(pieces) - 1 else (n + 1) * share)
                rows = slice(o * 256, o * 256 + PADDED)
                helds[slot][rows, :] = found if k == 0 else helds[slot][rows, :] + found
                if n == len(pieces) - 1:
                    wides[slot][...] = jnp.dot(ptable[...], chosen(plane_ref[b], 256, 0), preferred_element_type=jnp.float32).T
                    for m in range(BLOCK):
                        for t in range(COARSE):
                            code = codes[slot][(COPIED * LEAVES) // 128, m * COARSE + t]
                            picks[slot][COPIED * LEAVES + m * 8 + t] = flat[pl.ds(code, 2), :]

    def body(i, _):
        wcopy(i).wait()
        for slot in range(2):
            ccopy(2 * i + slot, slot).wait()
            block(2 * i + slot, slot)
            @pl.when(i < nit - 1)
            def _():
                ccopy(2 * i + slot + 2, slot).start()
        return 0

    lax.fori_loop(0, nit, body, 0)
    for n in range(COPIED + 2):
        multiply(NBLOCK - 1, 1, n)

    coarse_local = acc[288:296, 0:P_SIZE].astype(jnp.bfloat16)
    spread = [lax.dot_general(coarse_local, down_ref[c], NT, preferred_element_type=jnp.float32)[0:4] for c in range(8)]
    parent_local = (2.0 * acc[256:288, 0:P_SIZE] + jnp.concatenate(spread, axis=0)).astype(jnp.bfloat16)
    inherited = [lax.dot_general(parent_local, down_ref[c], NT, preferred_element_type=jnp.float32) for c in range(8)]
    far = 4.0 * acc[0:256, 0:P_SIZE] + jnp.concatenate(inherited, axis=0)
    out_ref[...] = far.T + 4.0 * turned[0:P_SIZE, :]


def main_call(codes, lanes, plane, w, own, ghosts, pown, coarse, down):
    vm = pl.BlockSpec(memory_space=pltpu.VMEM)
    anyspec = pl.BlockSpec(memory_space=pl.ANY)
    picked = COPIED * LEAVES + BLOCK * 8
    return pl.pallas_call(
        main_kernel,
        in_specs=[anyspec, vm, vm, anyspec] + [vm] * 11,
        out_specs=vm,
        out_shape=jax.ShapeDtypeStruct((P_SIZE, LEAVES), jnp.float32),
        scratch_shapes=[
            pltpu.VMEM((TABLE, 2, 128), jnp.float32),
            pltpu.VMEM((PADDED, 2048), jnp.bfloat16),
            pltpu.VMEM(((BLOCK - COPIED) * 256, LEAVES), jnp.float32), pltpu.VMEM(((BLOCK - COPIED) * 256, LEAVES), jnp.float32),
            pltpu.VMEM((256, 256), jnp.float32), pltpu.VMEM((256, 256), jnp.float32),
            pltpu.VMEM((256, 256), jnp.bfloat16),
            pltpu.VMEM((NBLOCK, PADDED, BLOCK * 256), jnp.bfloat16),
            pltpu.SMEM((16, 128), jnp.int32), pltpu.SMEM((16, 128), jnp.int32),
            pltpu.VMEM((picked, 2, 128), jnp.float32), pltpu.VMEM((picked, 2, 128), jnp.float32),
            pltpu.VMEM((ROWS, PADDED), jnp.float32),
            pltpu.VMEM((PADDED, LEAVES), jnp.float32),
            pltpu.SemaphoreType.DMA((NBLOCK // 2,)), pltpu.SemaphoreType.DMA((2,)),
        ],
        compiler_params=pltpu.CompilerParams(vmem_limit_bytes=58 << 20),
        cost_estimate=pl.CostEstimate(flops=2 * 296 * 48032 * 152, bytes_accessed=28_000_000, transcendentals=0),
    )(codes, lanes, plane, w, own, *ghosts, pown, coarse, down)


def tables(codes_leaf, valid_leaf, codes_parent, valid_parent, codes_coarse, valid_coarse):
    grow = ((0, BLOCK * NBLOCK - NOFF), (0, 0))
    lanes = jnp.pad(jnp.where(valid_leaf > 0, codes_leaf, -1), grow, constant_values=-1).reshape(NBLOCK, BLOCK, LEAVES)
    plane = jnp.pad(jnp.where(valid_parent > 0, codes_parent, -1), grow, constant_values=-1)
    plane = plane.reshape(NBLOCK, 1, BLOCK * PARENTS)
    coarse = jnp.pad(jnp.where(valid_coarse > 0, codes_coarse + 2048, ZERO), grow, constant_values=ZERO)
    coarse = jnp.pad(coarse.reshape(NBLOCK, 1, BLOCK * COARSE), ((0, 0), (0, 15 - 2 * COPIED), (0, 128 - BLOCK * COARSE)))
    rows = lanes[:, 0:COPIED].reshape(NBLOCK, COPIED * 2, 128)
    codes = 2 * jnp.concatenate([jnp.where(rows < 0, ZERO, rows), coarse], axis=1)
    return codes, lanes, plane


PBLOCK, STRIDE = 32, 136


def relay_kernel(f_ref, *refs):
    o_ref, halves = refs[-7], refs[-6:]

    def turn(k, p):
        first, last = k * 128, min(k * 128 + 128, NOFF)
        wide = f_ref[p, :, first:last].astype(jnp.float32)
        wide = jnp.concatenate([wide, jnp.zeros((256 - P_SIZE, last - first), jnp.float32)], axis=0).T
        for h in range(2):
            halves[2 * k + h][p * STRIDE:p * STRIDE + last - first, :] = wide[:, h * 128:h * 128 + 128]

    def give(o):
        for h in range(2):
            lane = (o % BLOCK) * 256 + h * 128
            rows = halves[2 * (o // 128) + h][pl.ds(o % 128, PBLOCK, stride=STRIDE), :]
            o_ref[o // BLOCK, :, lane:lane + 128] = rows.astype(jnp.bfloat16)

    always = pl.program_id(0) >= 0
    for k in range(4):
        for quarter in range(4):
            @pl.when(always)
            def _():
                if k < 3:
                    for p in range(quarter * PBLOCK // 4, (quarter + 1) * PBLOCK // 4):
                        turn(k, p)
                if k > 0:
                    for o in range((k - 1) * 128 + quarter * 32, min((k - 1) * 128 + quarter * 32 + 32, NOFF)):
                        give(o)
    o_ref[NBLOCK - 1, :, (NOFF % BLOCK) * 256:] = jnp.zeros((PBLOCK, (BLOCK - NOFF % BLOCK) * 256), jnp.bfloat16)


def relay(far, first, last, after):
    start, steps = first // PBLOCK, (last - first) // PBLOCK
    return pl.pallas_call(
        relay_kernel,
        grid=(steps,),
        in_specs=[pl.BlockSpec((PBLOCK, P_SIZE, NOFF), lambda i: (i + start, 0, 0))] + [pl.BlockSpec(memory_space=pl.ANY)] * len(after),
        out_specs=pl.BlockSpec((NBLOCK, PBLOCK, BLOCK * 256), lambda i: (0, i, 0)),
        out_shape=jax.ShapeDtypeStruct((NBLOCK, last - first, BLOCK * 256), jnp.bfloat16),
        scratch_shapes=[pltpu.VMEM((STRIDE * PBLOCK, 128), jnp.float32)] * 6,
        compiler_params=pltpu.CompilerParams(vmem_limit_bytes=58 << 20),
        cost_estimate=pl.CostEstimate(flops=0, bytes_accessed=9_000_000 * steps, transcendentals=0),
    )(jnp.transpose(far, (1, 2, 0)), *after)


def swapped(array, axis, distance):
    return lax.ppermute(array, axis, [(i, i ^ 1 << distance) for i in range(lax.axis_size(axis))])


def upward(matrices, children):
    groups = children.shape[1] // 8
    shaped = children.reshape(P_SIZE, 8, groups)
    return jnp.einsum("cpq,qcj->pj", matrices, shaped, preferred_element_type=jnp.float32).astype(jnp.bfloat16)


def shards(
    leaf_multipole,
    up_matrices,
    down_matrices,
    far_matrices,
    send_leaf,
    send_parent,
    codes_leaf,
    valid_leaf,
    codes_parent,
    valid_parent,
    codes_coarse,
    valid_coarse,
):
    own = leaf_multipole.T
    parent_mult = upward(up_matrices, leaf_multipole)
    parent_own = parent_mult.T
    coarse_mult = upward(up_matrices, parent_mult).T
    outgoing = jnp.concatenate(
        [
            own.at[send_leaf].get(mode="promise_in_bounds"),
            parent_own.at[send_parent].get(mode="promise_in_bounds"),
        ],
        axis=0,
    )
    ghosts = [swapped(outgoing, "gy", b) for b in range(5)] + [swapped(outgoing, "gx", b) for b in range(2)]
    spread = jnp.broadcast_to(coarse_mult[None], (128, 4, P_SIZE))
    coarse_all = lax.all_to_all(spread, ("gx", "gy"), 0, 0, tiled=True).reshape(512, P_SIZE)
    matrices = relay(far_matrices, 0, PADDED, ghosts[5:7])
    codes, lanes, plane = tables(codes_leaf, valid_leaf, codes_parent, valid_parent, codes_coarse, valid_coarse)
    return main_call(codes, lanes, plane, matrices, own, ghosts, parent_own, coarse_all, down_matrices)


def solution(mesh):
    spec = P(None, ("gx", "gy"))
    flat = P(("gx", "gy"))
    return jax.shard_map(
        shards,
        mesh=mesh,
        in_specs=(spec, P(), P(), P(), flat, flat, spec, spec, spec, spec, spec, spec),
        out_specs=spec,
        check_vma=False,
    )
```

```python
import jax
import jax.numpy as jnp
from jax import lax
from jax.experimental import pallas as pl
from jax.experimental.pallas import tpu as pltpu
from jax.sharding import PartitionSpec as P

NOFF, P_SIZE = 316, 152
BLOCK = 8
COPIED = 6
NBLOCK = 40
LEAVES, PARENTS, COARSE = 256, 32, 4
ROWS = 296
TABLE, ZERO = 2568, 2560
PADDED = 160
PIECE = 512
NT = (((1,), (1,)), ((), ()))


def main_kernel(codes_ref, lanes_ref, plane_ref, w_ref, own_ref, g0, g1, g2, g3, g4, g5, g6, pown_ref, coarse_ref,
                down_ref, out_ref, table, columns, h0, h1, v0, v1, ptable, wbuf, c0, c1, p0, p1, acc, turned, wsem, csem):
    nit = NBLOCK // 2
    codes, picks, helds, wides = (c0, c1), (p0, p1), (h0, h1), (v0, v1)

    def wcopy(i):
        return pltpu.make_async_copy(w_ref.at[pl.ds(i * 2, 2)], wbuf.at[pl.ds(i * 2, 2)], wsem.at[i])

    def ccopy(b, slot):
        return pltpu.make_async_copy(codes_ref.at[b], codes[slot], csem.at[slot])

    ccopy(0, 0).start()
    ccopy(1, 1).start()
    for i in range(nit):
        wcopy(i).start()
    flat = table.reshape(TABLE * 2, 128)

    def widened(rows):
        wide = rows.astype(jnp.float32)
        return jnp.concatenate([wide, jnp.zeros((rows.shape[0], 256 - P_SIZE), jnp.float32)], axis=1)

    def fill(base, wide):
        n = wide.shape[0]
        flat[pl.ds(2 * base, n, stride=2), :] = wide[:, :128]
        flat[pl.ds(2 * base + 1, n, stride=2), :] = wide[:, 128:]

    for ref in (h0, h1, p1.reshape((COPIED * LEAVES + BLOCK * 8) * 2, 128), v1):
        ref[...] = jnp.zeros(ref.shape, jnp.float32)
    for b, g in enumerate((own_ref, g0, g1, g2, g3, g4, g5, g6)):
        wide = widened(g[0:LEAVES, :])
        fill(LEAVES * b, wide)
        columns[:, LEAVES * b:LEAVES * (b + 1)] = wide.T[0:PADDED].astype(jnp.bfloat16)
    fill(2048, widened(coarse_ref[...]))
    flat[2 * ZERO:2 * TABLE, :] = jnp.zeros((2 * (TABLE - ZERO), 128), jnp.float32)
    parents = jnp.concatenate([pown_ref[...].astype(jnp.float32)] + [g[LEAVES:LEAVES + PARENTS, :].astype(jnp.float32) for g in (g0, g1, g2, g3, g4, g5, g6)], axis=0)
    ptable[...] = widened(parents).T.astype(jnp.bfloat16)
    acc[...] = jnp.zeros_like(acc)
    turned[...] = jnp.zeros_like(turned)
    for p in picks:
        for o in range(BLOCK):
            at = COPIED * LEAVES + o * 8
            p[at + COARSE:at + 8] = jnp.zeros((8 - COARSE, 2, 128), jnp.float32)

    def copy_rows(slot, start, stop):
        for word in range(start, stop):
            picks[slot][word] = flat[pl.ds(codes[slot][word // 128, word % 128], 2), :]

    def chosen(column, depth, base):
        hot = lax.broadcasted_iota(jnp.int32, (depth, column.shape[1]), 0) == column - base
        return jnp.where(hot, 1.0, 0.0).astype(jnp.bfloat16)

    def few(slot, o, h):
        at = COPIED * LEAVES + o * 8
        lines = picks[slot].reshape((COPIED * LEAVES + BLOCK * 8) * 2, 128)
        return [wides[slot][o * PARENTS:(o + 1) * PARENTS, h * 128:h * 128 + 128], lines[pl.ds(2 * at + h, 8, stride=2), :]]

    def multiply(b, slot, o):
        if o < COPIED:
            lines = picks[slot].reshape((COPIED * LEAVES + BLOCK * 8) * 2, 128)
            x = [jnp.concatenate([lines[pl.ds(o * LEAVES * 2 + h, LEAVES, stride=2), :]] + few(slot, o, h), axis=0).astype(jnp.bfloat16) for h in range(2)]
            acc[...] += lax.dot_general(jnp.concatenate(x, axis=1), wbuf[b, :, o * 256:(o + 1) * 256], NT, preferred_element_type=jnp.float32)
        elif o == COPIED:
            turned[...] += jnp.dot(wbuf[b, :, COPIED * 256:BLOCK * 256], helds[slot][...].astype(jnp.bfloat16), preferred_element_type=jnp.float32)
        else:
            x = [jnp.concatenate(few(slot, o, h), axis=0).astype(jnp.bfloat16) for o in range(COPIED, BLOCK) for h in range(2)]
            acc[LEAVES:ROWS, :] += lax.dot_general(jnp.concatenate(x, axis=1), wbuf[b, :, COPIED * 256:BLOCK * 256], NT, preferred_element_type=jnp.float32)

    pieces = [(o, k) for o in range(BLOCK - COPIED) for k in range(2048 // PIECE)]
    share = COPIED * LEAVES // len(pieces)

    def block(b, slot):
        for n, (o, k) in enumerate(pieces):
            @pl.when(b >= 0)
            def _():
                hot = chosen(lanes_ref[b, COPIED + o:COPIED + o + 1, :], PIECE, k * PIECE)
                found = jnp.dot(columns[:, k * PIECE:(k + 1) * PIECE], hot, preferred_element_type=jnp.float32)
                if n < COPIED + 2:
                    multiply(jnp.maximum(b - 1, 0), 1 - slot, n)
                copy_rows(slot, n * share, COPIED * LEAVES if n == len(pieces) - 1 else (n + 1) * share)
                rows = slice(o * 256, o * 256 + PADDED)
                helds[slot][rows, :] = found if k == 0 else helds[slot][rows, :] + found
                if n == len(pieces) - 1:
                    wides[slot][...] = jnp.dot(ptable[...], chosen(plane_ref[b], 256, 0), preferred_element_type=jnp.float32).T
                    for m in range(BLOCK):
                        for t in range(COARSE):
                            code = codes[slot][(COPIED * LEAVES) // 128, m * COARSE + t]
                            picks[slot][COPIED * LEAVES + m * 8 + t] = flat[pl.ds(code, 2), :]

    def body(i, _):
        wcopy(i).wait()
        for slot in range(2):
            ccopy(2 * i + slot, slot).wait()
            block(2 * i + slot, slot)
            @pl.when(i < nit - 1)
            def _():
                ccopy(2 * i + slot + 2, slot).start()
        return 0

    lax.fori_loop(0, nit, body, 0)
    for n in range(COPIED + 2):
        multiply(NBLOCK - 1, 1, n)

    coarse_local = acc[288:296, 0:P_SIZE].astype(jnp.bfloat16)
    spread = [lax.dot_general(coarse_local, down_ref[c], NT, preferred_element_type=jnp.float32)[0:4] for c in range(8)]
    parent_local = (2.0 * acc[256:288, 0:P_SIZE] + jnp.concatenate(spread, axis=0)).astype(jnp.bfloat16)
    inherited = [lax.dot_general(parent_local, down_ref[c], NT, preferred_element_type=jnp.float32) for c in range(8)]
    far = 4.0 * acc[0:256, 0:P_SIZE] + jnp.concatenate(inherited, axis=0)
    out_ref[...] = far.T + 4.0 * turned[0:P_SIZE, :]


def main_call(codes, lanes, plane, w, own, ghosts, pown, coarse, down):
    vm = pl.BlockSpec(memory_space=pltpu.VMEM)
    anyspec = pl.BlockSpec(memory_space=pl.ANY)
    picked = COPIED * LEAVES + BLOCK * 8
    return pl.pallas_call(
        main_kernel,
        in_specs=[anyspec, vm, vm, anyspec] + [vm] * 11,
        out_specs=vm,
        out_shape=jax.ShapeDtypeStruct((P_SIZE, LEAVES), jnp.float32),
        scratch_shapes=[
            pltpu.VMEM((TABLE, 2, 128), jnp.float32),
            pltpu.VMEM((PADDED, 2048), jnp.bfloat16),
            pltpu.VMEM(((BLOCK - COPIED) * 256, LEAVES), jnp.float32), pltpu.VMEM(((BLOCK - COPIED) * 256, LEAVES), jnp.float32),
            pltpu.VMEM((256, 256), jnp.float32), pltpu.VMEM((256, 256), jnp.float32),
            pltpu.VMEM((256, 256), jnp.bfloat16),
            pltpu.VMEM((NBLOCK, PADDED, BLOCK * 256), jnp.bfloat16),
            pltpu.SMEM((16, 128), jnp.int32), pltpu.SMEM((16, 128), jnp.int32),
            pltpu.VMEM((picked, 2, 128), jnp.float32), pltpu.VMEM((picked, 2, 128), jnp.float32),
            pltpu.VMEM((ROWS, PADDED), jnp.float32),
            pltpu.VMEM((PADDED, LEAVES), jnp.float32),
            pltpu.SemaphoreType.DMA((NBLOCK // 2,)), pltpu.SemaphoreType.DMA((2,)),
        ],
        compiler_params=pltpu.CompilerParams(vmem_limit_bytes=58 << 20),
        cost_estimate=pl.CostEstimate(flops=2 * 296 * 48032 * 152, bytes_accessed=28_000_000, transcendentals=0),
    )(codes, lanes, plane, w, own, *ghosts, pown, coarse, down)


def tables(codes_leaf, valid_leaf, codes_parent, valid_parent, codes_coarse, valid_coarse):
    grow = ((0, BLOCK * NBLOCK - NOFF), (0, 0))
    lanes = jnp.pad(jnp.where(valid_leaf > 0, codes_leaf, -1), grow, constant_values=-1).reshape(NBLOCK, BLOCK, LEAVES)
    plane = jnp.pad(jnp.where(valid_parent > 0, codes_parent, -1), grow, constant_values=-1)
    plane = plane.reshape(NBLOCK, 1, BLOCK * PARENTS)
    coarse = jnp.pad(jnp.where(valid_coarse > 0, codes_coarse + 2048, ZERO), grow, constant_values=ZERO)
    coarse = jnp.pad(coarse.reshape(NBLOCK, 1, BLOCK * COARSE), ((0, 0), (0, 15 - 2 * COPIED), (0, 128 - BLOCK * COARSE)))
    rows = lanes[:, 0:COPIED].reshape(NBLOCK, COPIED * 2, 128)
    codes = 2 * jnp.concatenate([jnp.where(rows < 0, ZERO, rows), coarse], axis=1)
    return codes, lanes, plane


PBLOCK, STRIDE = 32, 136


def relay_kernel(f_ref, *refs):
    o_ref, halves = refs[-7], refs[-6:]

    def turn(k, p):
        first, last = k * 128, min(k * 128 + 128, NOFF)
        wide = f_ref[p, :, first:last].astype(jnp.float32)
        wide = jnp.concatenate([wide, jnp.zeros((256 - P_SIZE, last - first), jnp.float32)], axis=0).T
        for h in range(2):
            halves[2 * k + h][p * STRIDE:p * STRIDE + last - first, :] = wide[:, h * 128:h * 128 + 128]

    def give(o):
        for h in range(2):
            lane = (o % BLOCK) * 256 + h * 128
            rows = halves[2 * (o // 128) + h][pl.ds(o % 128, PBLOCK, stride=STRIDE), :]
            o_ref[o // BLOCK, :, lane:lane + 128] = rows.astype(jnp.bfloat16)

    always = pl.program_id(0) >= 0
    for k in range(4):
        for quarter in range(4):
            @pl.when(always)
            def _():
                if k < 3:
                    for p in range(quarter * PBLOCK // 4, (quarter + 1) * PBLOCK // 4):
                        turn(k, p)
                if k > 0:
                    for o in range((k - 1) * 128 + quarter * 32, min((k - 1) * 128 + quarter * 32 + 32, NOFF)):
                        give(o)
    o_ref[NBLOCK - 1, :, (NOFF % BLOCK) * 256:] = jnp.zeros((PBLOCK, (BLOCK - NOFF % BLOCK) * 256), jnp.bfloat16)


def relay(far, first, last, after):
    start, steps = first // PBLOCK, (last - first) // PBLOCK
    return pl.pallas_call(
        relay_kernel,
        grid=(steps,),
        in_specs=[pl.BlockSpec((PBLOCK, P_SIZE, NOFF), lambda i: (i + start, 0, 0))] + [pl.BlockSpec(memory_space=pl.ANY)] * len(after),
        out_specs=pl.BlockSpec((NBLOCK, PBLOCK, BLOCK * 256), lambda i: (0, i, 0)),
        out_shape=jax.ShapeDtypeStruct((NBLOCK, last - first, BLOCK * 256), jnp.bfloat16),
        scratch_shapes=[pltpu.VMEM((STRIDE * PBLOCK, 128), jnp.float32)] * 6,
        compiler_params=pltpu.CompilerParams(vmem_limit_bytes=58 << 20),
        cost_estimate=pl.CostEstimate(flops=0, bytes_accessed=9_000_000 * steps, transcendentals=0),
    )(jnp.transpose(far, (1, 2, 0)), *after)


def swapped(array, axis, distance):
    return lax.ppermute(array, axis, [(i, i ^ 1 << distance) for i in range(lax.axis_size(axis))])


def upward(matrices, children):
    groups = children.shape[1] // 8
    shaped = children.reshape(P_SIZE, 8, groups)
    return jnp.einsum("cpq,qcj->pj", matrices, shaped, preferred_element_type=jnp.float32).astype(jnp.bfloat16)


def shards(
    leaf_multipole,
    up_matrices,
    down_matrices,
    far_matrices,
    send_leaf,
    send_parent,
    codes_leaf,
    valid_leaf,
    codes_parent,
    valid_parent,
    codes_coarse,
    valid_coarse,
):
    own = leaf_multipole.T
    parent_mult = upward(up_matrices, leaf_multipole)
    parent_own = parent_mult.T
    coarse_mult = upward(up_matrices, parent_mult).T
    outgoing = jnp.concatenate(
        [
            own.at[send_leaf].get(mode="promise_in_bounds", wrap_negative_indices=False),
            parent_own.at[send_parent].get(mode="promise_in_bounds", wrap_negative_indices=False),
        ],
        axis=0,
    )
    ghosts = [swapped(outgoing, "gy", b) for b in range(5)] + [swapped(outgoing, "gx", b) for b in range(2)]
    spread = jnp.broadcast_to(coarse_mult[None], (128, 4, P_SIZE))
    coarse_all = lax.all_to_all(spread, ("gx", "gy"), 0, 0, tiled=True).reshape(512, P_SIZE)
    matrices = relay(far_matrices, 0, PADDED, ghosts[5:7])
    codes, lanes, plane = tables(codes_leaf, valid_leaf, codes_parent, valid_parent, codes_coarse, valid_coarse)
    return main_call(codes, lanes, plane, matrices, own, ghosts, parent_own, coarse_all, down_matrices)


def solution(mesh):
    spec = P(None, ("gx", "gy"))
    flat = P(("gx", "gy"))
    return jax.shard_map(
        shards,
        mesh=mesh,
        in_specs=(spec, P(), P(), P(), flat, flat, spec, spec, spec, spec, spec, spec),
        out_specs=spec,
        check_vma=False,
    )
```

```python
import jax
import jax.numpy as jnp
from jax import lax
from jax.experimental import pallas as pl
from jax.experimental.pallas import tpu as pltpu
from jax.sharding import PartitionSpec as P

NOFF, P_SIZE = 316, 152
BLOCK = 8
COPIED = 6
NBLOCK = 40
LEAVES, PARENTS, COARSE = 256, 32, 4
ROWS = 296
TABLE, ZERO = 2568, 2560
PADDED = 160
PIECE = 512
NT = (((1,), (1,)), ((), ()))


def main_kernel(codes_ref, lanes_ref, plane_ref, w_ref, own_ref, g0, g1, g2, g3, g4, g5, g6, pown_ref, coarse_ref,
                down_ref, out_ref, table, columns, h0, h1, v0, v1, ptable, wbuf, c0, c1, p0, p1, acc, turned, wsem, csem):
    nit = NBLOCK // 2
    codes, picks, helds, wides = (c0, c1), (p0, p1), (h0, h1), (v0, v1)

    def wcopy(i):
        return pltpu.make_async_copy(w_ref.at[pl.ds(i * 2, 2)], wbuf.at[pl.ds(i * 2, 2)], wsem.at[i])

    def ccopy(b, slot):
        return pltpu.make_async_copy(codes_ref.at[b], codes[slot], csem.at[slot])

    ccopy(0, 0).start()
    ccopy(1, 1).start()
    for i in range(nit):
        wcopy(i).start()
    flat = table.reshape(TABLE * 2, 128)

    def widened(rows):
        wide = rows.astype(jnp.float32)
        return jnp.concatenate([wide, jnp.zeros((rows.shape[0], 256 - P_SIZE), jnp.float32)], axis=1)

    def fill(base, wide):
        n = wide.shape[0]
        flat[pl.ds(2 * base, n, stride=2), :] = wide[:, :128]
        flat[pl.ds(2 * base + 1, n, stride=2), :] = wide[:, 128:]

    for ref in (h0, h1, p1.reshape((COPIED * LEAVES + BLOCK * 8) * 2, 128), v1):
        ref[...] = jnp.zeros(ref.shape, jnp.float32)
    for b, g in enumerate((own_ref, g0, g1, g2, g3, g4, g5, g6)):
        wide = widened(g[0:LEAVES, :])
        fill(LEAVES * b, wide)
        columns[:, LEAVES * b:LEAVES * (b + 1)] = wide.T[0:PADDED].astype(jnp.bfloat16)
    fill(2048, widened(coarse_ref[...].astype(jnp.float32).reshape(512, P_SIZE)))
    flat[2 * ZERO:2 * TABLE, :] = jnp.zeros((2 * (TABLE - ZERO), 128), jnp.float32)
    parents = jnp.concatenate([pown_ref[...].astype(jnp.float32)] + [g[LEAVES:LEAVES + PARENTS, :].astype(jnp.float32) for g in (g0, g1, g2, g3, g4, g5, g6)], axis=0)
    ptable[...] = widened(parents).T.astype(jnp.bfloat16)
    acc[...] = jnp.zeros_like(acc)
    turned[...] = jnp.zeros_like(turned)
    for p in picks:
        for o in range(BLOCK):
            at = COPIED * LEAVES + o * 8
            p[at + COARSE:at + 8] = jnp.zeros((8 - COARSE, 2, 128), jnp.float32)

    def copy_rows(slot, start, stop):
        for word in range(start, stop):
            picks[slot][word] = flat[pl.ds(codes[slot][word // 128, word % 128], 2), :]

    def chosen(column, depth, base):
        hot = lax.broadcasted_iota(jnp.int32, (depth, column.shape[1]), 0) == column - base
        return jnp.where(hot, 1.0, 0.0).astype(jnp.bfloat16)

    def few(slot, o, h):
        at = COPIED * LEAVES + o * 8
        lines = picks[slot].reshape((COPIED * LEAVES + BLOCK * 8) * 2, 128)
        return [wides[slot][o * PARENTS:(o + 1) * PARENTS, h * 128:h * 128 + 128], lines[pl.ds(2 * at + h, 8, stride=2), :]]

    def multiply(b, slot, o):
        if o < COPIED:
            lines = picks[slot].reshape((COPIED * LEAVES + BLOCK * 8) * 2, 128)
            x = [jnp.concatenate([lines[pl.ds(o * LEAVES * 2 + h, LEAVES, stride=2), :]] + few(slot, o, h), axis=0).astype(jnp.bfloat16) for h in range(2)]
            acc[...] += lax.dot_general(jnp.concatenate(x, axis=1), wbuf[b, :, o * 256:(o + 1) * 256], NT, preferred_element_type=jnp.float32)
        elif o == COPIED:
            turned[...] += jnp.dot(wbuf[b, :, COPIED * 256:BLOCK * 256], helds[slot][...].astype(jnp.bfloat16), preferred_element_type=jnp.float32)
        else:
            x = [jnp.concatenate(few(slot, o, h), axis=0).astype(jnp.bfloat16) for o in range(COPIED, BLOCK) for h in range(2)]
            acc[LEAVES:ROWS, :] += lax.dot_general(jnp.concatenate(x, axis=1), wbuf[b, :, COPIED * 256:BLOCK * 256], NT, preferred_element_type=jnp.float32)

    pieces = [(o, k) for o in range(BLOCK - COPIED) for k in range(2048 // PIECE)]
    share = COPIED * LEAVES // len(pieces)

    def block(b, slot):
        for n, (o, k) in enumerate(pieces):
            @pl.when(b >= 0)
            def _():
                hot = chosen(lanes_ref[b, COPIED + o:COPIED + o + 1, :], PIECE, k * PIECE)
                found = jnp.dot(columns[:, k * PIECE:(k + 1) * PIECE], hot, preferred_element_type=jnp.float32)
                if n < COPIED + 2:
                    multiply(jnp.maximum(b - 1, 0), 1 - slot, n)
                copy_rows(slot, n * share, COPIED * LEAVES if n == len(pieces) - 1 else (n + 1) * share)
                rows = slice(o * 256, o * 256 + PADDED)
                helds[slot][rows, :] = found if k == 0 else helds[slot][rows, :] + found
                if n == len(pieces) - 1:
                    wides[slot][...] = jnp.dot(ptable[...], chosen(plane_ref[b], 256, 0), preferred_element_type=jnp.float32).T
                    for m in range(BLOCK):
                        for t in range(COARSE):
                            code = codes[slot][(COPIED * LEAVES) // 128, m * COARSE + t]
                            picks[slot][COPIED * LEAVES + m * 8 + t] = flat[pl.ds(code, 2), :]

    def body(i, _):
        wcopy(i).wait()
        for slot in range(2):
            ccopy(2 * i + slot, slot).wait()
            block(2 * i + slot, slot)
            @pl.when(i < nit - 1)
            def _():
                ccopy(2 * i + slot + 2, slot).start()
        return 0

    lax.fori_loop(0, nit, body, 0)
    for n in range(COPIED + 2):
        multiply(NBLOCK - 1, 1, n)

    coarse_local = acc[288:296, 0:P_SIZE].astype(jnp.bfloat16)
    spread = [lax.dot_general(coarse_local, down_ref[c], NT, preferred_element_type=jnp.float32)[0:4] for c in range(8)]
    parent_local = (2.0 * acc[256:288, 0:P_SIZE] + jnp.concatenate(spread, axis=0)).astype(jnp.bfloat16)
    inherited = [lax.dot_general(parent_local, down_ref[c], NT, preferred_element_type=jnp.float32) for c in range(8)]
    far = 4.0 * acc[0:256, 0:P_SIZE] + jnp.concatenate(inherited, axis=0)
    out_ref[...] = far.T + 4.0 * turned[0:P_SIZE, :]


def main_call(codes, lanes, plane, w, own, ghosts, pown, coarse, down):
    vm = pl.BlockSpec(memory_space=pltpu.VMEM)
    anyspec = pl.BlockSpec(memory_space=pl.ANY)
    picked = COPIED * LEAVES + BLOCK * 8
    return pl.pallas_call(
        main_kernel,
        in_specs=[anyspec, vm, vm, anyspec] + [vm] * 11,
        out_specs=vm,
        out_shape=jax.ShapeDtypeStruct((P_SIZE, LEAVES), jnp.float32),
        scratch_shapes=[
            pltpu.VMEM((TABLE, 2, 128), jnp.float32),
            pltpu.VMEM((PADDED, 2048), jnp.bfloat16),
            pltpu.VMEM(((BLOCK - COPIED) * 256, LEAVES), jnp.float32), pltpu.VMEM(((BLOCK - COPIED) * 256, LEAVES), jnp.float32),
            pltpu.VMEM((256, 256), jnp.float32), pltpu.VMEM((256, 256), jnp.float32),
            pltpu.VMEM((256, 256), jnp.bfloat16),
            pltpu.VMEM((NBLOCK, PADDED, BLOCK * 256), jnp.bfloat16),
            pltpu.SMEM((16, 128), jnp.int32), pltpu.SMEM((16, 128), jnp.int32),
            pltpu.VMEM((picked, 2, 128), jnp.float32), pltpu.VMEM((picked, 2, 128), jnp.float32),
            pltpu.VMEM((ROWS, PADDED), jnp.float32),
            pltpu.VMEM((PADDED, LEAVES), jnp.float32),
            pltpu.SemaphoreType.DMA((NBLOCK // 2,)), pltpu.SemaphoreType.DMA((2,)),
        ],
        compiler_params=pltpu.CompilerParams(vmem_limit_bytes=58 << 20),
        cost_estimate=pl.CostEstimate(flops=2 * 296 * 48032 * 152, bytes_accessed=28_000_000, transcendentals=0),
    )(codes, lanes, plane, w, own, *ghosts, pown, coarse, down)


def tables(codes_leaf, valid_leaf, codes_parent, valid_parent, codes_coarse, valid_coarse):
    grow = ((0, BLOCK * NBLOCK - NOFF), (0, 0))
    lanes = jnp.pad(jnp.where(valid_leaf > 0, codes_leaf, -1), grow, constant_values=-1).reshape(NBLOCK, BLOCK, LEAVES)
    plane = jnp.pad(jnp.where(valid_parent > 0, codes_parent, -1), grow, constant_values=-1)
    plane = plane.reshape(NBLOCK, 1, BLOCK * PARENTS)
    coarse = jnp.pad(jnp.where(valid_coarse > 0, codes_coarse + 2048, ZERO), grow, constant_values=ZERO)
    coarse = jnp.pad(coarse.reshape(NBLOCK, 1, BLOCK * COARSE), ((0, 0), (0, 15 - 2 * COPIED), (0, 128 - BLOCK * COARSE)))
    rows = lanes[:, 0:COPIED].reshape(NBLOCK, COPIED * 2, 128)
    codes = 2 * jnp.concatenate([jnp.where(rows < 0, ZERO, rows), coarse], axis=1)
    return codes, lanes, plane


PBLOCK, STRIDE = 32, 136


def relay_kernel(f_ref, *refs):
    o_ref, halves = refs[-7], refs[-6:]

    def turn(k, p):
        first, last = k * 128, min(k * 128 + 128, NOFF)
        wide = f_ref[p, :, first:last].astype(jnp.float32)
        wide = jnp.concatenate([wide, jnp.zeros((256 - P_SIZE, last - first), jnp.float32)], axis=0).T
        for h in range(2):
            halves[2 * k + h][p * STRIDE:p * STRIDE + last - first, :] = wide[:, h * 128:h * 128 + 128]

    def give(o):
        for h in range(2):
            lane = (o % BLOCK) * 256 + h * 128
            rows = halves[2 * (o // 128) + h][pl.ds(o % 128, PBLOCK, stride=STRIDE), :]
            o_ref[o // BLOCK, :, lane:lane + 128] = rows.astype(jnp.bfloat16)

    always = pl.program_id(0) >= 0
    for k in range(4):
        for quarter in range(4):
            @pl.when(always)
            def _():
                if k < 3:
                    for p in range(quarter * PBLOCK // 4, (quarter + 1) * PBLOCK // 4):
                        turn(k, p)
                if k > 0:
                    for o in range((k - 1) * 128 + quarter * 32, min((k - 1) * 128 + quarter * 32 + 32, NOFF)):
                        give(o)
    o_ref[NBLOCK - 1, :, (NOFF % BLOCK) * 256:] = jnp.zeros((PBLOCK, (BLOCK - NOFF % BLOCK) * 256), jnp.bfloat16)


def relay(far, first, last, after):
    start, steps = first // PBLOCK, (last - first) // PBLOCK
    return pl.pallas_call(
        relay_kernel,
        grid=(steps,),
        in_specs=[pl.BlockSpec((PBLOCK, P_SIZE, NOFF), lambda i: (i + start, 0, 0))] + [pl.BlockSpec(memory_space=pl.ANY)] * len(after),
        out_specs=pl.BlockSpec((NBLOCK, PBLOCK, BLOCK * 256), lambda i: (0, i, 0)),
        out_shape=jax.ShapeDtypeStruct((NBLOCK, last - first, BLOCK * 256), jnp.bfloat16),
        scratch_shapes=[pltpu.VMEM((STRIDE * PBLOCK, 128), jnp.float32)] * 6,
        compiler_params=pltpu.CompilerParams(vmem_limit_bytes=58 << 20),
        cost_estimate=pl.CostEstimate(flops=0, bytes_accessed=9_000_000 * steps, transcendentals=0),
    )(jnp.transpose(far, (1, 2, 0)), *after)


def swapped(array, axis, distance):
    return lax.ppermute(array, axis, [(i, i ^ 1 << distance) for i in range(lax.axis_size(axis))])


def upward(matrices, children):
    groups = children.shape[1] // 8
    shaped = children.reshape(P_SIZE, 8, groups)
    return jnp.einsum("cpq,qcj->pj", matrices, shaped, preferred_element_type=jnp.float32).astype(jnp.bfloat16)


def shards(
    leaf_multipole,
    up_matrices,
    down_matrices,
    far_matrices,
    send_leaf,
    send_parent,
    codes_leaf,
    valid_leaf,
    codes_parent,
    valid_parent,
    codes_coarse,
    valid_coarse,
):
    own = leaf_multipole.T
    parent_mult = upward(up_matrices, leaf_multipole)
    parent_own = parent_mult.T
    coarse_mult = upward(up_matrices, parent_mult).T
    outgoing = jnp.concatenate(
        [
            own.at[send_leaf].get(mode="promise_in_bounds", wrap_negative_indices=False),
            parent_own.at[send_parent].get(mode="promise_in_bounds", wrap_negative_indices=False),
        ],
        axis=0,
    )
    ghosts = [swapped(outgoing, "gy", b) for b in range(5)] + [swapped(outgoing, "gx", b) for b in range(2)]
    spread = jnp.broadcast_to(coarse_mult[None], (128, 4, P_SIZE))
    coarse_all = lax.all_to_all(spread, ("gx", "gy"), 0, 0, tiled=True)
    matrices = relay(far_matrices, 0, PADDED, ghosts[5:7])
    codes, lanes, plane = tables(codes_leaf, valid_leaf, codes_parent, valid_parent, codes_coarse, valid_coarse)
    return main_call(codes, lanes, plane, matrices, own, ghosts, parent_own, coarse_all, down_matrices)


def solution(mesh):
    spec = P(None, ("gx", "gy"))
    flat = P(("gx", "gy"))
    return jax.shard_map(
        shards,
        mesh=mesh,
        in_specs=(spec, P(), P(), P(), flat, flat, spec, spec, spec, spec, spec, spec),
        out_specs=spec,
        check_vma=False,
    )
```
